512 devices in a mesh: grp: 16 (over z_hi, y), seq: 32 (over x, z_lo, core).
Axes of the slice: x: 4, y: 4, z: 16 (z_hi: 4, z_lo: 4; z = z_hi * 4 + z_lo), core: 2. Of those that a mesh axis runs over, the one named last changes fastest.
Arguments:
- tokens: bfloat16 [65536, 768], P(('grp', 'seq')), may hold values from -40 to 40
- tile_pos: int32 [2, 65536], P(None, ('grp', 'seq')), may hold values from 0 to 1023
- w_qkv: bfloat16 [768, 2304], replicated, may hold values from -1 to 1
- w_out: bfloat16 [768, 768], P('grp'), may hold values from -0.21875 to 0.21875
Outputs:
- output: bfloat16 [65536, 768], P(('grp', 'seq'))
The draws below stay inside these ranges and needn't reach their ends.
All inputs are finite; a program needn't handle non-finite values.
Results may differ from the reference program's by a relative error of at most 0.011.
Values may be sent and summed in bfloat16 or wider, within the bound.
A program may use at most 64 MiB of HBM per device.

```python
import jax
import jax.numpy as jnp
import numpy as np
from jax import lax

D = 768
H = 16
TOKENS = 65536
SPARSE = 512
R1 = 8
R2 = 32
R3 = 128


def draw_tokens(key, part):
    key = jax.random.fold_in(key, 11)
    return jax.random.normal(key, (TOKENS, D), jnp.float32).astype(jnp.bfloat16)


def draw_w_qkv(key, part):
    key = jax.random.fold_in(key, 23)
    fresh = jax.random.normal(key, (D, 3 * D), jnp.float32) * D ** (-0.5)
    return jnp.concatenate([2.0 * fresh[:, :D], fresh[:, D:]], axis=1).astype(jnp.bfloat16)


def place_ends(drawn, stream_key, least, high):
    index_at = [jax.random.randint(jax.random.fold_in(stream_key, axis), (), 0, length) for axis, length in enumerate(drawn.shape)]
    longest = drawn.shape.index(max(drawn.shape))
    next_to = index_at[:longest] + [(index_at[longest] + 1) % drawn.shape[longest]] + index_at[longest + 1:]
    return drawn.at[tuple(index_at)].set(least).at[tuple(next_to)].set(high)


def block_scale(rng, shape, cuts, smallest, top_value):
    gain, own = 1.0, jax.random.fold_in(rng, 6)
    for position, parts in cuts:
        heights = jnp.exp(jax.random.uniform(jax.random.fold_in(own, position), (parts,), jnp.float32, smallest / len(cuts), top_value / len(cuts)))
        gain = gain * jnp.repeat(heights, shape[position] // parts).reshape([-1 if axis == position else 1 for axis in range(len(shape))])
    return gain


def centred(rng, extent, width, most, shards=(), kind=jnp.bfloat16):
    drawn = jax.random.normal(rng, extent, jnp.float32) * width
    if len(shards) > 0:
        drawn = block_scale(rng, extent, shards, -0.22, 0.18) * drawn
    return jnp.clip(drawn, min=-most, max=most).astype(kind)


def setup_inputs(seed: int = 0) -> dict:
    splits = jax.random.split(jax.random.key(seed), 5)
    return {
        "tokens": draw_tokens(jax.random.fold_in(splits[4], 71), 0),
        "tile_pos": place_ends(jax.random.randint(splits[1], (2, TOKENS), 0, 1024), jax.random.fold_in(splits[1], 1), 0, 1023).astype(jnp.int32),
        "w_qkv": draw_w_qkv(jax.random.fold_in(splits[4], 71), 0),
        "w_out": centred(splits[3], (D, D), D ** -0.5, 0.21875, ((0, 16),)),
    }


def embed(tile_pos, feat_width):
    quarter = feat_width // 4
    omega = 10000.0 ** (-jnp.arange(quarter, dtype=jnp.float32) / quarter)
    across = tile_pos[0].astype(jnp.float32)[:, None] * omega[None, :]
    downward = tile_pos[1].astype(jnp.float32)[:, None] * omega[None, :]
    return jnp.concatenate([jnp.sin(across), jnp.cos(across), jnp.sin(downward), jnp.cos(downward)], axis=1)


def attend(queries, keys_all, values_all):
    score_scale = queries.shape[2] ** -0.5
    scores = jnp.einsum("qhd,khd->hqk", queries.astype(jnp.float32), keys_all.astype(jnp.float32)) * score_scale
    top = jnp.max(scores, axis=2)
    weights = jnp.exp(scores - top[:, :, None])
    total = jnp.sum(weights, axis=2)
    rounded = lax.optimization_barrier(weights.astype(jnp.bfloat16)).astype(jnp.float32)
    mixed = jnp.einsum("hqk,khd->qhd", rounded, values_all.astype(jnp.float32))
    return top.T, total.T, mixed


def branch(queries, keys_all, values_all, segment, dilation):
    total_rows = queries.shape[0]
    head_count = queries.shape[1]
    head_dim = queries.shape[2]
    count = total_rows // segment
    span = segment // dilation
    head_ids = np.arange(head_count)
    offsets = head_ids % dilation

    def pick(array):
        return array.reshape(count, span, dilation, head_count, head_dim)[:, :, offsets, head_ids]

    def one_segment(triple):
        return attend(triple[0], triple[1], triple[2])

    top, total, mixed = lax.map(one_segment, (pick(queries), pick(keys_all), pick(values_all)))

    def place(array):
        tail = array.shape[3:]
        full = jnp.zeros((count, span, dilation, head_count) + tail, jnp.float32)
        return full.at[:, :, offsets, head_ids].set(array).reshape((total_rows, head_count) + tail)

    member = np.arange(dilation)[:, None] == offsets[None, :]
    member = np.broadcast_to(member[None, None], (count, span, dilation, head_count)).reshape(total_rows, head_count)
    return place(top), place(total), place(mixed), jnp.asarray(member)


def reference(tokens, tile_pos, w_qkv, w_out):
    head_dim = D // H
    embedded = (tokens.astype(jnp.float32) + embed(tile_pos, D)).astype(jnp.bfloat16)
    qkv = jnp.dot(embedded, w_qkv, preferred_element_type=jnp.float32).astype(jnp.bfloat16)
    queries = qkv[:, :D].reshape(TOKENS, H, head_dim)
    keys_all = qkv[:, D:2 * D].reshape(TOKENS, H, head_dim)
    values_all = qkv[:, 2 * D:].reshape(TOKENS, H, head_dim)
    layout = ((SPARSE, 1), (SPARSE * R1, R1), (SPARSE * R2, R2), (SPARSE * R3, R3))
    results = [branch(queries, keys_all, values_all, segment, dilation) for segment, dilation in layout]
    best = results[0][0]
    for item in results[1:]:
        best = jnp.maximum(best, jnp.where(item[3], item[0], best))
    numer = jnp.zeros((TOKENS, H, head_dim), jnp.float32)
    denom = jnp.zeros((TOKENS, H), jnp.float32)
    for item in results:
        factor = jnp.where(item[3], jnp.exp(jnp.where(item[3], item[0], best) - best), 0.0)
        numer = numer + factor[..., None] * item[2]
        denom = denom + factor * item[1]
    attended = (numer / denom[..., None]).reshape(TOKENS, D).astype(jnp.bfloat16)
    return jnp.dot(attended, w_out, preferred_element_type=jnp.float32).astype(jnp.bfloat16)
```

```python
import jax
import jax.numpy as jnp
import numpy as np
from jax import lax
from jax.experimental import pallas as pl
from jax.experimental.pallas import tpu as pltpu
from jax.sharding import PartitionSpec as P

MESH = pl.DeviceIdType.MESH
F32 = jnp.float32
BF16 = jnp.bfloat16
ROWS = 128
WIDTH = 768
HEADS = 16
LOG2E = 1.4426950408889634
SCALE = 48 ** (-0.5) * LOG2E


def iota(shape, axis):
    return lax.broadcasted_iota(jnp.int32, shape, axis)


def dot(a, b):
    return jnp.dot(a, b, preferred_element_type=F32)


def dot_nt(a, b):
    return lax.dot_general(a, b, (((1,), (1,)), ((), ())), preferred_element_type=F32)


def row_order(p):
    return p // 16 + 8 * ((p % 4) * 4 + (p % 16) // 4)


def sine(angle, quarter_turns):
    turns = jnp.floor(angle * (2.0 / np.pi) + 0.5)
    rest = ((angle - turns * 1.5703125) - turns * 4.837512969970703125e-4) - turns * 7.54978995489188216e-8
    quadrant = turns.astype(jnp.int32) + quarter_turns
    sq = rest * rest
    sin_part = rest + rest * sq * (-1.6666654611e-1 + sq * (8.3321608736e-3 - sq * 1.9515295891e-4))
    cos_part = 1.0 - 0.5 * sq + sq * sq * (
        4.166664568298827e-2 + sq * (-1.388731625493765e-3 + sq * 2.443315711809948e-5)
    )
    value = jnp.where((quadrant & 1) == 1, cos_part, sin_part)
    return jnp.where((quadrant & 2) == 2, -value, value)


def soft(scores):
    top = jnp.max(scores, axis=1, keepdims=True)
    return top, jnp.exp2((scores - top) * SCALE)


def merge(a, l, b, m):
    gap = m - l
    share = 1.0 / (1.0 + jnp.exp2(-gap))
    both = jnp.maximum(l, m) + jnp.log2(1.0 + jnp.exp2(-jnp.abs(gap)))
    return a + (b - a) * share, both


def attend(queries, keys_values):
    top, weights = soft(dot_nt(queries, keys_values))
    mixed = dot(weights.astype(BF16), keys_values)
    total = mixed[:, 96:97]
    return mixed * (1.0 / total), top * SCALE + jnp.log2(total)


def kernel(
    tok_hbm, pos_hbm, omega_hbm, wqkv_hbm, wout_hbm, out_ref,
    tok, pos, omega, wq, emb, q_own, kv_all, msg, recv_a, kv3, far, q3, out2, msg_c, recv_c,
    att, lse, wall,
    load_sem, emb_send, emb_recv, a_send, a_recv, relay_send, relay_recv,
    kv3_send, kv3_recv, far_send, far_recv, o2_send, o2_recv, c_send, c_recv,
    w1_send, w1_recv, w2_send, w2_recv, w3_send, w3_recv,
):
    g = lax.axis_index("grp")
    s = lax.axis_index("seq")
    core = s % 2
    chip = s // 2
    x = s // 8
    zh = g // 4
    y = g % 4
    sibling = s + 1 - 2 * core
    across = s + 2 - 4 * (chip % 2)
    half_cols = pl.ds(pl.multiple_of(384 * core, 128), 384)

    def remote(src, dst, send_sem, recv_sem, grp, seq):
        return pltpu.make_async_remote_copy(
            src_ref=src, dst_ref=dst, send_sem=send_sem, recv_sem=recv_sem,
            device_id=(grp, seq), device_id_type=MESH,
        )

    def each(low, high, body):
        def step(i, carry):
            body(i)
            return carry
        lax.fori_loop(low, high, step, 0)

    load_tok = pltpu.make_async_copy(tok_hbm, tok, load_sem.at[0])
    load_pos = pltpu.make_async_copy(pos_hbm, pos, load_sem.at[1])
    load_omega = pltpu.make_async_copy(omega_hbm, omega, load_sem.at[2])
    load_wq = [
        pltpu.make_async_copy(
            wqkv_hbm.at[:, pl.ds(WIDTH * i, WIDTH)], wq.at[:, pl.ds(WIDTH * i, WIDTH)], load_sem.at[3 + i]
        )
        for i in range(3)
    ]
    load_tok.start()
    load_pos.start()
    load_omega.start()
    for item in load_wq:
        item.start()

    barrier = pltpu.get_barrier_semaphore()

    def greet(grp, seq):
        pl.semaphore_signal(barrier, inc=1, device_id=(grp, seq), device_id_type=MESH)

    @pl.when(core == 1)
    def _():
        each(1, 32, lambda k: greet(g, (s + k) % 32))
        each(1, 16, lambda k: greet((g + k) % 16, s))
        each(0, 9, lambda k: greet(zh * 4 + (y + 1 + k % 3) % 4, ((x + 1 + k // 3) % 4) * 8 + s % 8))

    @pl.when(core == 0)
    def _():
        each(0, 16, lambda k: greet(g, 2 * k + 1))
        greet(g, across)
        each(1, 4, lambda k: greet((g + 4 * k) % 16, s))
        each(1, 16, lambda k: greet(zh * 4 + (y + k % 4) % 4, ((x + k // 4) % 4) * 8 + s % 8))

    load_tok.wait()
    load_pos.wait()
    load_omega.wait()
    order = (row_order(iota((ROWS, ROWS), 0)) == iota((ROWS, ROWS), 1)).astype(F32)
    place = pos[...].astype(F32)
    pos_x = jnp.sum(order * place[0:1, :], axis=1, keepdims=True)
    pos_y = jnp.sum(order * place[1:2, :], axis=1, keepdims=True)
    order_bf = order.astype(BF16)
    for i in range(6):
        cols = slice(128 * i, 128 * i + 128)
        lane = iota((1, 128), 1) + 128 * i
        spot = pos_x if i < 3 else pos_y
        turn = ((lane % 384) >= 192).astype(jnp.int32)
        value = sine(spot * omega[0:1, cols], turn)
        emb[0, :, cols] = (dot(order_bf, tok[:, cols]) + value).astype(BF16)

    @pl.when(core == 1)
    def _():
        pl.semaphore_wait(barrier, 55)

    @pl.when(core == 0)
    def _():
        pl.semaphore_wait(barrier, 35)

    send_across = remote(emb.at[0], emb.at[2], emb_send.at[0], emb_recv.at[0], g, across)
    send_sibling = remote(emb.at[0], emb.at[1], emb_send.at[1], emb_recv.at[1], g, sibling)
    send_on = remote(emb.at[2], emb.at[3], emb_send.at[2], emb_recv.at[2], g, sibling)
    send_across.start()
    send_sibling.start()

    for i in range(3):
        load_wq[i].wait()
        for j in range(3):
            part = dot(emb[0], wq[:, WIDTH * i + 256 * j : WIDTH * i + 256 * j + 256]).astype(BF16)
            if i == 0:
                q_own[:, 256 * j : 256 * j + 256] = part
            else:
                first = WIDTH * (i - 1) + 256 * j
                kv_all[0:ROWS, first : first + 256] = part

    lane128 = iota((1, 128), 1)
    for rho in range(8):
        base = 128 * (rho >= 3)
        off = 48 * rho - base
        src_row = iota((256, 128), 0)
        dst_lane = iota((256, 128), 1)
        put_first = ((src_row == dst_lane + off) & (dst_lane < 48)).astype(F32).astype(BF16)
        put_second = (
            (src_row == dst_lane - 48 + off) & (dst_lane >= 48) & (dst_lane < 96)
        ).astype(F32).astype(BF16)
        rows = slice(16 * rho, 16 * rho + 16)
        for e in range(2):
            h = rho + 8 * e
            w0 = 384 * e + base
            q_part = dot(q_own[rows, w0 : w0 + 256], put_first)
            kv_part = dot(kv_all[rows, w0 : w0 + 256], put_first) + dot(
                kv_all[rows, WIDTH + w0 : WIDTH + w0 + 256], put_second
            )
            kv_part = jnp.where(lane128 >= 96, 1.0, kv_part)
            msg[h, :, 0:128] = kv_part.astype(BF16)
            msg[h, :, 128:256] = q_part.astype(BF16)

    def a_copy(k):
        h = (chip + k) % 16
        return remote(msg.at[h], recv_a.at[s], a_send.at[k], a_recv, g, 2 * h + 1)

    a_local = pltpu.make_async_copy(msg.at[chip], recv_a.at[s], a_recv)

    @pl.when(core == 1)
    def _():
        a_local.start()

    each(1, 16, lambda k: a_copy(k).start())

    @pl.when(core == 0)
    def _():
        a_copy(0).start()

    my_part = wall.at[zh, y, x % 3, :, half_cols]

    def w1_copy(k):
        return remote(my_part, my_part, w1_send.at[k], w1_recv.at[zh], (g + 4 * k) % 16, s)

    @pl.when(x < 3)
    def _():
        load = pltpu.make_async_copy(
            wout_hbm.at[pl.ds(pl.multiple_of(16 * (x % 3), 16), 16), half_cols], my_part, load_sem.at[6]
        )
        load.start()
        load.wait()
        each(1, 4, lambda k: w1_copy(k).start())

    def other_rows(slot):
        for j in range(6):
            cols = slice(256 * j, 256 * j + 256)
            kv_all[ROWS * slot : ROWS * slot + ROWS, cols] = dot(
                emb[slot], wq[:, WIDTH + 256 * j : WIDTH + 256 * j + 256]
            ).astype(BF16)

    send_sibling.wait_recv()
    other_rows(1)
    send_across.wait_recv()
    send_on.start()
    other_rows(2)
    send_on.wait_recv()
    other_rows(3)

    e_own = chip // 8
    relay = remote(recv_a, recv_a, relay_send, relay_recv, g, sibling)
    give = remote(out2, out2, o2_send, o2_recv, g, sibling)

    def kv3_copy(k):
        block = kv3.at[y]
        return remote(block, block, kv3_send.at[k], kv3_recv.at[y], zh * 4 + (y + k) % 4, s)

    def far_copy(k):
        return remote(
            kv3.at[y, pl.ds(0, 32)], far.at[g], far_send.at[k], far_recv.at[g],
            ((zh + k // 4) % 4) * 4 + k % 4, s,
        )

    @pl.when(core == 1)
    def _():
        pltpu.make_async_copy(recv_a, recv_a, a_recv).wait()
        relay.start()
        spot = iota((128, 512), 0)
        col = iota((128, 512), 1)
        pick = ((spot % 32) * 16 + 4 * e_own + spot // 32 == col).astype(F32).astype(BF16)
        chosen = dot(pick, recv_a[...].reshape(512, 256)).astype(BF16)
        kv3[y] = chosen[:, 0:128]
        q3[...] = chosen[:, 128:256]
        each(4, 16, lambda k: far_copy(k).start())
        each(1, 4, lambda k: kv3_copy(k).start())

    @pl.when(core == 0)
    def _():
        relay.wait_recv()

        def block(i, carry):
            rows = pl.ds(pl.multiple_of(128 * i, 128), 128)
            flat = recv_a[...].reshape(512, 256)
            queries = recv_a[pl.ds(8 * i, 8)][:, :, 128:256].reshape(128, 128)
            mixed, level = attend(queries, flat[:, 0:128])
            out2[rows, :] = jnp.where(lane128 < 48, level, mixed)
            return carry

        lax.fori_loop(0, 4, block, 0)
        give.start()

    def first_branch(rho, carry):
        b = (rho + 5) // 8
        off = 48 * rho - 128 * b
        lane = iota((1, 256), 1)
        mine = (lane >= off) & (lane < off + 48)
        keep = mine.astype(F32).astype(BF16)
        for e in range(2):
            w0 = 384 * e + 128 * b
            win = pl.ds(pl.multiple_of(w0, 128), 256)
            win_v = pl.ds(pl.multiple_of(WIDTH + w0, 128), 256)
            top, weights = soft(dot_nt(q_own[:, win] * keep, kv_all[:, win]))
            total = jnp.sum(weights, axis=1, keepdims=True)
            mixed = dot(weights.astype(BF16), kv_all[:, win_v]) * (1.0 / total)
            att[:, win] = jnp.where(mine, mixed, att[:, win])
            lse[rho + 8 * e] = jnp.broadcast_to(top * SCALE + jnp.log2(total), (ROWS, 128))
        return carry

    lax.fori_loop(0, 4, first_branch, 0)

    @pl.when(x < 3)
    def _():
        each(1, 4, lambda k: pltpu.make_async_copy(my_part, my_part, w1_recv.at[(zh + k) % 4]).wait())

    my_column = wall.at[:, y, x % 3, :, half_cols]

    def w2_copy(k):
        return remote(
            my_column, my_column, w2_send.at[k], w2_recv.at[(x % 3) * 4 + y],
            zh * 4 + (y + k % 4) % 4, ((x + k // 4) % 4) * 8 + s % 8,
        )

    @pl.when(x < 3)
    def _():
        each(1, 16, lambda k: w2_copy(k).start())

    def c_copy(k):
        there = (s + k) % 32
        return remote(msg_c.at[there], recv_c.at[chip], c_send.at[k], c_recv, g, there)

    @pl.when(core == 1)
    def _():
        each(1, 4, lambda k: pltpu.make_async_copy(kv3.at[0], kv3.at[0], kv3_recv.at[(y + k) % 4]).wait())
        mixed3, level3 = attend(q3[...], kv3[...].reshape(512, 128))
        each(4, 16, lambda k: pltpu.make_async_copy(
            far.at[0], far.at[0], far_recv.at[((zh + k // 4) % 4) * 4 + k % 4]).wait())
        for k in range(4):
            far[zh * 4 + k] = kv3[k, 0:32, :]
        mixed4, level4 = attend(q3[0:32, :], far[...].reshape(512, 128))
        give.wait_recv()
        for m in range(4):
            a, l = mixed3[32 * m : 32 * m + 32], level3[32 * m : 32 * m + 32]
            if m == 0:
                a, l = merge(a, l, mixed4, level4)
            rows = pl.ds(4 * e_own + m, 32, stride=16)
            held = out2[rows, :]
            a, l = merge(held, held[:, 0:1], a, l)
            out2[rows, :] = jnp.where(lane128 < 48, l, a)
        done = out2[...]
        level = done[:, 0:1]
        high = level.astype(BF16).astype(F32)
        mid = (level - high).astype(BF16).astype(F32)
        low = level - high - mid
        coded = jnp.where(lane128 == 0, high, jnp.where(lane128 == 1, mid, jnp.where(lane128 == 2, low, done)))
        msg_c[...] = coded.astype(BF16).reshape(32, 16, 128)
        pltpu.make_async_copy(msg_c.at[s], recv_c.at[chip], c_recv).start()
        each(1, 32, lambda k: c_copy(k).start())

    lax.fori_loop(4, 8, first_branch, 0)

    def from_plane(i):
        @pl.when(i != x * 4 + y)
        def _():
            pltpu.make_async_copy(my_column, my_column, w2_recv.at[i]).wait()

    each(0, 12, from_plane)
    w3 = remote(
        wall.at[:, :, :, :, half_cols], wall.at[:, :, :, :, half_cols], w3_send, w3_recv, g, sibling
    )
    w3.start()

    pltpu.make_async_copy(recv_c, recv_c, c_recv).wait()
    for rho in range(8):
        base = 128 * (rho >= 3)
        off = 48 * rho - base
        src_row = iota((128, 256), 0)
        dst_lane = iota((128, 256), 1)
        put_back = ((src_row - 48 + off == dst_lane) & (src_row >= 48) & (src_row < 96)).astype(F32).astype(BF16)
        add_up = (src_row < 3).astype(F32).astype(BF16)
        lane = iota((1, 256), 1)
        mine = (lane >= off) & (lane < off + 48)
        rows = slice(16 * rho, 16 * rho + 16)
        for e in range(2):
            h = rho + 8 * e
            w0 = 384 * e + base
            other = dot(recv_c[h], put_back)
            level = dot(recv_c[h], add_up)
            own_level = lse[h, rows, 0:1]
            held = att[rows, w0 : w0 + 256]
            share = 1.0 / (1.0 + jnp.exp2(own_level - level))
            att[rows, w0 : w0 + 256] = jnp.where(mine, held + (other - held) * share, held)

    back = (row_order(iota((ROWS, ROWS), 1)) == iota((ROWS, ROWS), 0)).astype(F32).astype(BF16)
    attended = dot(back, att[...].astype(BF16)).astype(BF16)
    w3.wait_recv()
    for j in range(3):
        cols = slice(256 * j, 256 * j + 256)
        out_ref[:, cols] = dot(attended, wall[:, :, :, :, cols].reshape(WIDTH, 256)).astype(BF16)

    send_across.wait_send()
    send_sibling.wait_send()
    send_on.wait_send()
    each(1, 16, lambda k: a_copy(k).wait_send())

    @pl.when(core == 0)
    def _():
        a_copy(0).wait_send()
        give.wait_send()

    @pl.when(core == 1)
    def _():
        relay.wait_send()
        each(1, 4, lambda k: kv3_copy(k).wait_send())
        each(4, 16, lambda k: far_copy(k).wait_send())
        each(1, 32, lambda k: c_copy(k).wait_send())

    @pl.when(x < 3)
    def _():
        each(1, 4, lambda k: w1_copy(k).wait_send())
        each(1, 16, lambda k: w2_copy(k).wait_send())

    w3.wait_send()


def shards(tokens, tile_pos, w_qkv, w_out):
    omega = 10000.0 ** (-(np.arange(WIDTH) % (WIDTH // 4)).astype(np.float64) / (WIDTH // 4))
    omega = jnp.asarray(np.broadcast_to(omega.astype(np.float32), (8, WIDTH)))
    dma = pltpu.SemaphoreType.DMA
    anywhere = pl.BlockSpec(memory_space=pl.ANY)
    return pl.pallas_call(
        kernel,
        out_shape=jax.ShapeDtypeStruct((ROWS, WIDTH), BF16),
        in_specs=[anywhere] * 5,
        out_specs=pl.BlockSpec(memory_space=pltpu.VMEM),
        scratch_shapes=[
            pltpu.VMEM((ROWS, WIDTH), BF16),
            pltpu.VMEM((2, ROWS), jnp.int32),
            pltpu.VMEM((8, WIDTH), F32),
            pltpu.VMEM((WIDTH, 3 * WIDTH), BF16),
            pltpu.VMEM((4, ROWS, WIDTH), BF16),
            pltpu.VMEM((ROWS, WIDTH), BF16),
            pltpu.VMEM((4 * ROWS, 2 * WIDTH), BF16),
            pltpu.VMEM((HEADS, 16, 256), BF16),
            pltpu.VMEM((32, 16, 256), BF16),
            pltpu.VMEM((4, 128, 128), BF16),
            pltpu.VMEM((16, 32, 128), BF16),
            pltpu.VMEM((128, 128), BF16),
            pltpu.VMEM((512, 128), F32),
            pltpu.VMEM((32, 16, 128), BF16),
            pltpu.VMEM((HEADS, 16, 128), BF16),
            pltpu.VMEM((ROWS, WIDTH), F32),
            pltpu.VMEM((HEADS, ROWS, 128), F32),
            pltpu.VMEM((4, 4, 3, 16, WIDTH), BF16),
            dma((7,)), dma((3,)), dma((3,)), dma((16,)), dma, dma, dma,
            dma((4,)), dma((4,)), dma((16,)), dma((16,)), dma, dma, dma((32,)), dma,
            dma((4,)), dma((4,)), dma((16,)), dma((12,)), dma, dma,
        ],
        compiler_params=pltpu.CompilerParams(
            collective_id=0, has_side_effects=True, vmem_limit_bytes=40 * 1024 * 1024
        ),
        name="dilated_attention",
    )(tokens, tile_pos, omega, w_qkv, w_out)


def solution(mesh):
    placed = (P(("grp", "seq"), None), P(None, ("grp", "seq")), P(), P("grp", None))
    return jax.shard_map(
        shards, mesh=mesh, in_specs=placed, out_specs=P(("grp", "seq"), None), check_vma=False
    )
```

```python
import jax
import jax.numpy as jnp
import numpy as np
from jax import lax
from jax.experimental import pallas as pl
from jax.experimental.pallas import tpu as pltpu
from jax.sharding import PartitionSpec as P

MESH = pl.DeviceIdType.MESH
F32 = jnp.float32
BF16 = jnp.bfloat16
ROWS = 128
WIDTH = 768
HEADS = 16
LOG2E = 1.4426950408889634
SCALE = 48 ** (-0.5) * LOG2E


def iota(shape, axis):
    return lax.broadcasted_iota(jnp.int32, shape, axis)


def dot(a, b):
    return jnp.dot(a, b, preferred_element_type=F32)


def dot_nt(a, b):
    return lax.dot_general(a, b, (((1,), (1,)), ((), ())), preferred_element_type=F32)


def row_order(p):
    return p // 16 + 8 * ((p % 4) * 4 + (p % 16) // 4)


def omega(lane):
    j = lane % 192
    rate = jnp.ones(lane.shape, F32)
    for bit in range(8):
        rate = jnp.where((j // 2**bit) % 2 == 1, rate * float(10000.0 ** (-(2**bit) / 192)), rate)
    return rate


def sine(angle, quarter_turns):
    turns = jnp.floor(angle * (2.0 / np.pi) + 0.5)
    rest = ((angle - turns * 1.5703125) - turns * 4.837512969970703125e-4) - turns * 7.54978995489188216e-8
    quadrant = turns.astype(jnp.int32) + quarter_turns
    sq = rest * rest
    sin_part = rest + rest * sq * (-1.6666654611e-1 + sq * (8.3321608736e-3 - sq * 1.9515295891e-4))
    cos_part = 1.0 - 0.5 * sq + sq * sq * (
        4.166664568298827e-2 + sq * (-1.388731625493765e-3 + sq * 2.443315711809948e-5)
    )
    value = jnp.where((quadrant & 1) == 1, cos_part, sin_part)
    return jnp.where((quadrant & 2) == 2, -value, value)


def soft(scores):
    top = jnp.max(scores, axis=1, keepdims=True)
    return top, jnp.exp2((scores - top) * SCALE)


def merge(a, l, b, m):
    gap = m - l
    share = 1.0 / (1.0 + jnp.exp2(-gap))
    both = jnp.maximum(l, m) + jnp.log2(1.0 + jnp.exp2(-jnp.abs(gap)))
    return a + (b - a) * share, both


def attend(queries, keys_values):
    top, weights = soft(dot_nt(queries, keys_values))
    mixed = dot(weights.astype(BF16), keys_values)
    total = mixed[:, 96:97]
    return mixed * (1.0 / total), top * SCALE + jnp.log2(total)


def kernel(
    tok_hbm, pos_hbm, wqkv_hbm, wout_hbm, out_ref,
    tok, pos, wq, emb, q_own, kv_all, msg, recv_a, kv3, far, q3, out2, msg_c, recv_c,
    att, lse, wall,
    load_sem, emb_send, emb_recv, a_send, a_recv, relay_send, relay_recv,
    kv3_send, kv3_recv, far_send, far_recv, o2_send, o2_recv, c_send, c_recv,
    w1_send, w1_recv, w2_send, w2_recv, w3_send, w3_recv,
):
    g = lax.axis_index("grp")
    s = lax.axis_index("seq")
    core = s % 2
    chip = s // 2
    x = s // 8
    zh = g // 4
    y = g % 4
    sibling = s + 1 - 2 * core
    across = s + 2 - 4 * (chip % 2)
    half_cols = pl.ds(pl.multiple_of(384 * core, 128), 384)

    def remote(src, dst, send_sem, recv_sem, grp, seq):
        return pltpu.make_async_remote_copy(
            src_ref=src, dst_ref=dst, send_sem=send_sem, recv_sem=recv_sem,
            device_id=(grp, seq), device_id_type=MESH,
        )

    def each(low, high, body):
        def step(i, carry):
            body(i)
            return carry
        lax.fori_loop(low, high, step, 0)

    load_tok = pltpu.make_async_copy(tok_hbm, tok, load_sem.at[0])
    load_pos = pltpu.make_async_copy(pos_hbm, pos, load_sem.at[1])
    load_wq = [
        pltpu.make_async_copy(
            wqkv_hbm.at[:, pl.ds(WIDTH * i, WIDTH)], wq.at[:, pl.ds(WIDTH * i, WIDTH)], load_sem.at[2 + i]
        )
        for i in range(3)
    ]
    load_tok.start()
    load_pos.start()
    for item in load_wq:
        item.start()

    barrier = pltpu.get_barrier_semaphore()

    def greet(grp, seq):
        pl.semaphore_signal(barrier, inc=1, device_id=(grp, seq), device_id_type=MESH)

    @pl.when(core == 1)
    def _():
        each(1, 32, lambda k: greet(g, (s + k) % 32))
        each(1, 16, lambda k: greet((g + k) % 16, s))
        each(0, 9, lambda k: greet(zh * 4 + (y + 1 + k % 3) % 4, ((x + 1 + k // 3) % 4) * 8 + s % 8))

    @pl.when(core == 0)
    def _():
        each(0, 16, lambda k: greet(g, 2 * k + 1))
        greet(g, across)
        each(1, 4, lambda k: greet((g + 4 * k) % 16, s))
        each(1, 16, lambda k: greet(zh * 4 + (y + k % 4) % 4, ((x + k // 4) % 4) * 8 + s % 8))

    load_tok.wait()
    load_pos.wait()
    order = (row_order(iota((ROWS, ROWS), 0)) == iota((ROWS, ROWS), 1)).astype(F32)
    place = pos[...].astype(F32)
    pos_x = jnp.sum(order * place[0:1, :], axis=1, keepdims=True)
    pos_y = jnp.sum(order * place[1:2, :], axis=1, keepdims=True)
    order_bf = order.astype(BF16)
    for i in range(6):
        cols = slice(128 * i, 128 * i + 128)
        lane = iota((1, 128), 1) + 128 * i
        spot = pos_x if i < 3 else pos_y
        turn = ((lane % 384) >= 192).astype(jnp.int32)
        value = sine(spot * omega(lane), turn)
        emb[0, :, cols] = (dot(order_bf, tok[:, cols]) + value).astype(BF16)

    @pl.when(core == 1)
    def _():
        pl.semaphore_wait(barrier, 55)

    @pl.when(core == 0)
    def _():
        pl.semaphore_wait(barrier, 35)

    send_across = remote(emb.at[0], emb.at[2], emb_send.at[0], emb_recv.at[0], g, across)
    send_sibling = remote(emb.at[0], emb.at[1], emb_send.at[1], emb_recv.at[1], g, sibling)
    send_on = remote(emb.at[2], emb.at[3], emb_send.at[2], emb_recv.at[2], g, sibling)
    send_across.start()
    send_sibling.start()

    for i in range(3):
        load_wq[i].wait()
        for j in range(3):
            part = dot(emb[0], wq[:, WIDTH * i + 256 * j : WIDTH * i + 256 * j + 256]).astype(BF16)
            if i == 0:
                q_own[:, 256 * j : 256 * j + 256] = part
            else:
                first = WIDTH * (i - 1) + 256 * j
                kv_all[0:ROWS, first : first + 256] = part

    lane128 = iota((1, 128), 1)
    for rho in range(8):
        base = 128 * (rho >= 3)
        off = 48 * rho - base
        src_row = iota((256, 128), 0)
        dst_lane = iota((256, 128), 1)
        put_first = ((src_row == dst_lane + off) & (dst_lane < 48)).astype(F32).astype(BF16)
        put_second = (
            (src_row == dst_lane - 48 + off) & (dst_lane >= 48) & (dst_lane < 96)
        ).astype(F32).astype(BF16)
        rows = slice(16 * rho, 16 * rho + 16)
        for e in range(2):
            h = rho + 8 * e
            w0 = 384 * e + base
            q_part = dot(q_own[rows, w0 : w0 + 256], put_first)
            kv_part = dot(kv_all[rows, w0 : w0 + 256], put_first) + dot(
                kv_all[rows, WIDTH + w0 : WIDTH + w0 + 256], put_second
            )
            kv_part = jnp.where(lane128 >= 96, 1.0, kv_part)
            msg[h, :, 0:128] = kv_part.astype(BF16)
            msg[h, :, 128:256] = q_part.astype(BF16)

    def a_copy(k):
        h = (chip + k) % 16
        return remote(msg.at[h], recv_a.at[s], a_send.at[k], a_recv, g, 2 * h + 1)

    a_local = pltpu.make_async_copy(msg.at[chip], recv_a.at[s], a_recv)

    @pl.when(core == 1)
    def _():
        a_local.start()

    each(1, 16, lambda k: a_copy(k).start())

    @pl.when(core == 0)
    def _():
        a_copy(0).start()

    my_part = wall.at[zh, y, x % 3, :, half_cols]

    def w1_copy(k):
        return remote(my_part, my_part, w1_send.at[k], w1_recv.at[zh], (g + 4 * k) % 16, s)

    @pl.when(x < 3)
    def _():
        load = pltpu.make_async_copy(
            wout_hbm.at[pl.ds(pl.multiple_of(16 * (x % 3), 16), 16), half_cols], my_part, load_sem.at[5]
        )
        load.start()
        load.wait()
        each(1, 4, lambda k: w1_copy(k).start())

    def other_rows(slot):
        for j in range(6):
            cols = slice(256 * j, 256 * j + 256)
            kv_all[ROWS * slot : ROWS * slot + ROWS, cols] = dot(
                emb[slot], wq[:, WIDTH + 256 * j : WIDTH + 256 * j + 256]
            ).astype(BF16)

    send_sibling.wait_recv()
    other_rows(1)
    send_across.wait_recv()
    send_on.start()
    other_rows(2)
    send_on.wait_recv()
    other_rows(3)

    e_own = chip // 8
    relay = remote(recv_a, recv_a, relay_send, relay_recv, g, sibling)
    give = remote(out2, out2, o2_send, o2_recv, g, sibling)

    def kv3_copy(k):
        block = kv3.at[y]
        return remote(block, block, kv3_send.at[k], kv3_recv.at[y], zh * 4 + (y + k) % 4, s)

    def far_copy(k):
        return remote(
            kv3.at[y, pl.ds(0, 32)], far.at[g], far_send.at[k], far_recv.at[g],
            ((zh + k // 4) % 4) * 4 + k % 4, s,
        )

    @pl.when(core == 1)
    def _():
        pltpu.make_async_copy(recv_a, recv_a, a_recv).wait()
        relay.start()
        spot = iota((128, 512), 0)
        col = iota((128, 512), 1)
        pick = ((spot % 32) * 16 + 4 * e_own + spot // 32 == col).astype(F32).astype(BF16)
        chosen = dot(pick, recv_a[...].reshape(512, 256)).astype(BF16)
        kv3[y] = chosen[:, 0:128]
        q3[...] = chosen[:, 128:256]
        each(4, 16, lambda k: far_copy(k).start())
        each(1, 4, lambda k: kv3_copy(k).start())

    @pl.when(core == 0)
    def _():
        relay.wait_recv()

        def block(i, carry):
            rows = pl.ds(pl.multiple_of(128 * i, 128), 128)
            flat = recv_a[...].reshape(512, 256)
            queries = recv_a[pl.ds(8 * i, 8)][:, :, 128:256].reshape(128, 128)
            mixed, level = attend(queries, flat[:, 0:128])
            out2[rows, :] = jnp.where(lane128 < 48, level, mixed)
            return carry

        lax.fori_loop(0, 4, block, 0)
        give.start()

    def first_branch(rho, carry):
        b = (rho + 5) // 8
        off = 48 * rho - 128 * b
        lane = iota((1, 256), 1)
        mine = (lane >= off) & (lane < off + 48)
        keep = mine.astype(F32).astype(BF16)
        for e in range(2):
            w0 = 384 * e + 128 * b
            win = pl.ds(pl.multiple_of(w0, 128), 256)
            win_v = pl.ds(pl.multiple_of(WIDTH + w0, 128), 256)
            top, weights = soft(dot_nt(q_own[:, win] * keep, kv_all[:, win]))
            total = jnp.sum(weights, axis=1, keepdims=True)
            mixed = dot(weights.astype(BF16), kv_all[:, win_v]) * (1.0 / total)
            att[:, win] = jnp.where(mine, mixed, att[:, win])
            lse[rho + 8 * e] = jnp.broadcast_to(top * SCALE + jnp.log2(total), (ROWS, 128))
        return carry

    lax.fori_loop(0, 4, first_branch, 0)

    @pl.when(x < 3)
    def _():
        each(1, 4, lambda k: pltpu.make_async_copy(my_part, my_part, w1_recv.at[(zh + k) % 4]).wait())

    my_column = wall.at[:, y, x % 3, :, half_cols]

    def w2_copy(k):
        return remote(
            my_column, my_column, w2_send.at[k], w2_recv.at[(x % 3) * 4 + y],
            zh * 4 + (y + k % 4) % 4, ((x + k // 4) % 4) * 8 + s % 8,
        )

    @pl.when(x < 3)
    def _():
        each(1, 16, lambda k: w2_copy(k).start())

    def c_copy(k):
        there = (s + k) % 32
        return remote(msg_c.at[there], recv_c.at[chip], c_send.at[k], c_recv, g, there)

    @pl.when(core == 1)
    def _():
        each(1, 4, lambda k: pltpu.make_async_copy(kv3.at[0], kv3.at[0], kv3_recv.at[(y + k) % 4]).wait())
        mixed3, level3 = attend(q3[...], kv3[...].reshape(512, 128))
        each(4, 16, lambda k: pltpu.make_async_copy(
            far.at[0], far.at[0], far_recv.at[((zh + k // 4) % 4) * 4 + k % 4]).wait())
        for k in range(4):
            far[zh * 4 + k] = kv3[k, 0:32, :]
        mixed4, level4 = attend(q3[0:32, :], far[...].reshape(512, 128))
        give.wait_recv()
        for m in range(4):
            a, l = mixed3[32 * m : 32 * m + 32], level3[32 * m : 32 * m + 32]
            if m == 0:
                a, l = merge(a, l, mixed4, level4)
            rows = pl.ds(4 * e_own + m, 32, stride=16)
            held = out2[rows, :]
            a, l = merge(held, held[:, 0:1], a, l)
            out2[rows, :] = jnp.where(lane128 < 48, l, a)
        done = out2[...]
        level = done[:, 0:1]
        high = level.astype(BF16).astype(F32)
        mid = (level - high).astype(BF16).astype(F32)
        low = level - high - mid
        coded = jnp.where(lane128 == 0, high, jnp.where(lane128 == 1, mid, jnp.where(lane128 == 2, low, done)))
        msg_c[...] = coded.astype(BF16).reshape(32, 16, 128)
        pltpu.make_async_copy(msg_c.at[s], recv_c.at[chip], c_recv).start()
        each(1, 32, lambda k: c_copy(k).start())

    lax.fori_loop(4, 8, first_branch, 0)

    def from_plane(i):
        @pl.when(i != x * 4 + y)
        def _():
            pltpu.make_async_copy(my_column, my_column, w2_recv.at[i]).wait()

    each(0, 12, from_plane)
    w3 = remote(
        wall.at[:, :, :, :, half_cols], wall.at[:, :, :, :, half_cols], w3_send, w3_recv, g, sibling
    )
    w3.start()

    pltpu.make_async_copy(recv_c, recv_c, c_recv).wait()
    for rho in range(8):
        base = 128 * (rho >= 3)
        off = 48 * rho - base
        src_row = iota((128, 256), 0)
        dst_lane = iota((128, 256), 1)
        put_back = ((src_row - 48 + off == dst_lane) & (src_row >= 48) & (src_row < 96)).astype(F32).astype(BF16)
        add_up = (src_row < 3).astype(F32).astype(BF16)
        lane = iota((1, 256), 1)
        mine = (lane >= off) & (lane < off + 48)
        rows = slice(16 * rho, 16 * rho + 16)
        for e in range(2):
            h = rho + 8 * e
            w0 = 384 * e + base
            other = dot(recv_c[h], put_back)
            level = dot(recv_c[h], add_up)
            own_level = lse[h, rows, 0:1]
            held = att[rows, w0 : w0 + 256]
            share = 1.0 / (1.0 + jnp.exp2(own_level - level))
            att[rows, w0 : w0 + 256] = jnp.where(mine, held + (other - held) * share, held)

    back = (row_order(iota((ROWS, ROWS), 1)) == iota((ROWS, ROWS), 0)).astype(F32).astype(BF16)
    attended = dot(back, att[...].astype(BF16)).astype(BF16)
    w3.wait_recv()
    for j in range(3):
        cols = slice(256 * j, 256 * j + 256)
        out_ref[:, cols] = dot(attended, wall[:, :, :, :, cols].reshape(WIDTH, 256)).astype(BF16)

    send_across.wait_send()
    send_sibling.wait_send()
    send_on.wait_send()
    each(1, 16, lambda k: a_copy(k).wait_send())

    @pl.when(core == 0)
    def _():
        a_copy(0).wait_send()
        give.wait_send()

    @pl.when(core == 1)
    def _():
        relay.wait_send()
        each(1, 4, lambda k: kv3_copy(k).wait_send())
        each(4, 16, lambda k: far_copy(k).wait_send())
        each(1, 32, lambda k: c_copy(k).wait_send())

    @pl.when(x < 3)
    def _():
        each(1, 4, lambda k: w1_copy(k).wait_send())
        each(1, 16, lambda k: w2_copy(k).wait_send())

    w3.wait_send()


def shards(tokens, tile_pos, w_qkv, w_out):
    dma = pltpu.SemaphoreType.DMA
    in_hbm = pl.BlockSpec(memory_space=pltpu.HBM)
    return pl.pallas_call(
        kernel,
        out_shape=jax.ShapeDtypeStruct((ROWS, WIDTH), BF16),
        in_specs=[in_hbm] * 4,
        out_specs=pl.BlockSpec(memory_space=pltpu.VMEM),
        scratch_shapes=[
            pltpu.VMEM((ROWS, WIDTH), BF16),
            pltpu.VMEM((2, ROWS), jnp.int32),
            pltpu.VMEM((WIDTH, 3 * WIDTH), BF16),
            pltpu.VMEM((4, ROWS, WIDTH), BF16),
            pltpu.VMEM((ROWS, WIDTH), BF16),
            pltpu.VMEM((4 * ROWS, 2 * WIDTH), BF16),
            pltpu.VMEM((HEADS, 16, 256), BF16),
            pltpu.VMEM((32, 16, 256), BF16),
            pltpu.VMEM((4, 128, 128), BF16),
            pltpu.VMEM((16, 32, 128), BF16),
            pltpu.VMEM((128, 128), BF16),
            pltpu.VMEM((512, 128), F32),
            pltpu.VMEM((32, 16, 128), BF16),
            pltpu.VMEM((HEADS, 16, 128), BF16),
            pltpu.VMEM((ROWS, WIDTH), F32),
            pltpu.VMEM((HEADS, ROWS, 128), F32),
            pltpu.VMEM((4, 4, 3, 16, WIDTH), BF16),
            dma((6,)), dma((3,)), dma((3,)), dma((16,)), dma, dma, dma,
            dma((4,)), dma((4,)), dma((16,)), dma((16,)), dma, dma, dma((32,)), dma,
            dma((4,)), dma((4,)), dma((16,)), dma((12,)), dma, dma,
        ],
        compiler_params=pltpu.CompilerParams(
            collective_id=0, has_side_effects=True, vmem_limit_bytes=60 * 1024 * 1024
        ),
        name="dilated_attention",
    )(tokens, tile_pos, w_qkv, w_out)


def solution(mesh):
    placed = (P(("grp", "seq"), None), P(None, ("grp", "seq")), P(), P("grp", None))
    return jax.shard_map(
        shards, mesh=mesh, in_specs=placed, out_specs=P(("grp", "seq"), None), check_vma=False
    )
```

```python
import jax
import jax.numpy as jnp
import numpy as np
from jax import lax
from jax.experimental import pallas as pl
from jax.experimental.pallas import tpu as pltpu
from jax.sharding import PartitionSpec as P

MESH = pl.DeviceIdType.MESH
F32 = jnp.float32
BF16 = jnp.bfloat16
ROWS = 128
WIDTH = 768
HEADS = 16
LOG2E = 1.4426950408889634
SCALE = 48 ** (-0.5) * LOG2E


def iota(shape, axis):
    return lax.broadcasted_iota(jnp.int32, shape, axis)


def dot(a, b):
    return jnp.dot(a, b, preferred_element_type=F32)


def dot_nt(a, b):
    return lax.dot_general(a, b, (((1,), (1,)), ((), ())), preferred_element_type=F32)


def row_order(p):
    return p // 16 + 8 * ((p % 4) * 4 + (p % 16) // 4)


def omega(lane):
    j = lane % 192
    rate = jnp.ones(lane.shape, F32)
    for bit in range(8):
        rate = jnp.where((j // 2**bit) % 2 == 1, rate * float(10000.0 ** (-(2**bit) / 192)), rate)
    return rate


def sine(angle, quarter_turns):
    turns = jnp.floor(angle * (2.0 / np.pi) + 0.5)
    rest = ((angle - turns * 1.5703125) - turns * 4.837512969970703125e-4) - turns * 7.54978995489188216e-8
    quadrant = turns.astype(jnp.int32) + quarter_turns
    sq = rest * rest
    sin_part = rest + rest * sq * (-1.6666654611e-1 + sq * (8.3321608736e-3 - sq * 1.9515295891e-4))
    cos_part = 1.0 - 0.5 * sq + sq * sq * (
        4.166664568298827e-2 + sq * (-1.388731625493765e-3 + sq * 2.443315711809948e-5)
    )
    value = jnp.where((quadrant & 1) == 1, cos_part, sin_part)
    return jnp.where((quadrant & 2) == 2, -value, value)


def soft(scores):
    top = jnp.max(scores, axis=1, keepdims=True)
    return top, jnp.exp2((scores - top) * SCALE)


def merge(a, l, b, m):
    gap = m - l
    share = 1.0 / (1.0 + jnp.exp2(-gap))
    both = jnp.maximum(l, m) + jnp.log2(1.0 + jnp.exp2(-jnp.abs(gap)))
    return a + (b - a) * share, both


def attend(queries, keys_values):
    top, weights = soft(dot_nt(queries, keys_values))
    mixed = dot(weights.astype(BF16), keys_values)
    total = mixed[:, 96:97]
    return mixed * (1.0 / total), top * SCALE + jnp.log2(total)


def kernel(
    tok_hbm, pos_hbm, wqkv_hbm, wout_hbm, out_ref,
    tok, pos, wq, emb, q_own, kv_all, msg, recv_a, kv3, far, q3, out2, msg_c, recv_c,
    att, lse, wall,
    load_sem, emb_send, emb_recv, a_send, a_recv, relay_send, relay_recv,
    kv3_send, kv3_recv, far_send, far_recv, o2_send, o2_recv, c_send, c_recv,
    w1_send, w1_recv, w2_send, w2_recv, w3_send, w3_recv, past, past_too,
):
    g = lax.axis_index("grp")
    s = lax.axis_index("seq")
    core = s % 2
    chip = s // 2
    x = s // 8
    zh = g // 4
    y = g % 4
    sibling = s + 1 - 2 * core
    across = s + 2 - 4 * (chip % 2)
    half_cols = pl.ds(pl.multiple_of(384 * core, 128), 384)

    def remote(src, dst, send_sem, recv_sem, grp, seq):
        return pltpu.make_async_remote_copy(
            src_ref=src, dst_ref=dst, send_sem=send_sem, recv_sem=recv_sem,
            device_id=(grp, seq), device_id_type=MESH,
        )

    def each(low, high, body):
        def step(i, carry):
            body(i)
            return carry
        lax.fori_loop(low, high, step, 0)

    def seat(k):
        return ((x + 2 + k // 4) % 4) * 4 + (chip + k) % 4

    load_tok = pltpu.make_async_copy(tok_hbm, tok, load_sem.at[0])
    load_pos = pltpu.make_async_copy(pos_hbm, pos, load_sem.at[1])
    load_wq = [
        pltpu.make_async_copy(
            wqkv_hbm.at[:, pl.ds(WIDTH * i, WIDTH)], wq.at[:, pl.ds(WIDTH * i, WIDTH)], load_sem.at[2 + i]
        )
        for i in range(3)
    ]
    load_tok.start()
    load_pos.start()
    for item in load_wq:
        item.start()

    my_part = wall.at[zh, y, x % 3, :, half_cols]
    load_wout = pltpu.make_async_copy(
        wout_hbm.at[pl.ds(pl.multiple_of(16 * (x % 3), 16), 16), half_cols], my_part, load_sem.at[5]
    )

    @pl.when(x < 3)
    def _():
        load_wout.start()

    barrier = pltpu.get_barrier_semaphore()

    def greet(grp, seq):
        pl.semaphore_signal(barrier, inc=1, device_id=(grp, seq), device_id_type=MESH)

    @pl.when(core == 1)
    def _():
        greet((g + 4) % 16, s)
        greet((g + 12) % 16, s)
        each(1, 32, lambda k: greet(g, (s + k) % 32))
        each(1, 4, lambda k: greet(zh * 4 + (y + k) % 4, s))

    @pl.when(core == 0)
    def _():
        greet((g + 4) % 16, s)
        greet((g + 12) % 16, s)
        each(0, 16, lambda k: greet(g, 2 * k + 1))
        greet(g, across)
        each(1, 16, lambda k: greet(zh * 4 + (y + k % 4) % 4, ((x + k // 4) % 4) * 8 + s % 8))

    load_tok.wait()
    load_pos.wait()
    order = (row_order(iota((ROWS, ROWS), 0)) == iota((ROWS, ROWS), 1)).astype(F32)
    place = pos[...].astype(F32)
    pos_x = jnp.sum(order * place[0:1, :], axis=1, keepdims=True)
    pos_y = jnp.sum(order * place[1:2, :], axis=1, keepdims=True)
    order_bf = order.astype(BF16)
    for i in range(6):
        cols = slice(128 * i, 128 * i + 128)
        lane = iota((1, 128), 1) + 128 * i
        spot = pos_x if i < 3 else pos_y
        turn = ((lane % 384) >= 192).astype(jnp.int32)
        value = sine(spot * omega(lane), turn)
        emb[0, :, cols] = (dot(order_bf, tok[:, cols]) + value).astype(BF16)

    for i in range(3):
        load_wq[i].wait()
        for j in range(3):
            part = dot(emb[0], wq[:, WIDTH * i + 256 * j : WIDTH * i + 256 * j + 256]).astype(BF16)
            if i == 0:
                q_own[:, 256 * j : 256 * j + 256] = part
            else:
                first = WIDTH * (i - 1) + 256 * j
                kv_all[0:ROWS, first : first + 256] = part

    lane128 = iota((1, 128), 1)
    for rho in range(8):
        base = 128 * (rho >= 3)
        off = 48 * rho - base
        src_row = iota((256, 128), 0)
        dst_lane = iota((256, 128), 1)
        put_first = ((src_row == dst_lane + off) & (dst_lane < 48)).astype(F32).astype(BF16)
        put_second = (
            (src_row == dst_lane - 48 + off) & (dst_lane >= 48) & (dst_lane < 96)
        ).astype(F32).astype(BF16)
        rows = slice(16 * rho, 16 * rho + 16)
        for e in range(2):
            h = rho + 8 * e
            w0 = 384 * e + base
            q_part = dot(q_own[rows, w0 : w0 + 256], put_first)
            kv_part = dot(kv_all[rows, w0 : w0 + 256], put_first) + dot(
                kv_all[rows, WIDTH + w0 : WIDTH + w0 + 256], put_second
            )
            kv_part = jnp.where(lane128 >= 96, 1.0, kv_part)
            msg[h, :, 0:128] = kv_part.astype(BF16)
            msg[h, :, 128:256] = q_part.astype(BF16)

    @pl.when(core == 1)
    def _():
        pl.semaphore_wait(barrier, 36)

    @pl.when(core == 0)
    def _():
        pl.semaphore_wait(barrier, 34)

    def a_copy(k):
        h = seat(k)
        return remote(msg.at[h], recv_a.at[s], a_send.at[k], a_recv, g, 2 * h + 1)

    a_local = pltpu.make_async_copy(msg.at[chip], recv_a.at[s], a_recv)

    def a_all(act):
        each(0, 8, lambda k: act(a_copy(k)))
        each(9, 16, lambda k: act(a_copy(k)))

        @pl.when(core == 0)
        def _():
            act(a_copy(8))

    a_all(lambda c: c.start())

    @pl.when(core == 1)
    def _():
        a_local.start()

    send_across = remote(emb.at[0], emb.at[2], emb_send.at[0], emb_recv.at[0], g, across)
    send_sibling = remote(emb.at[0], emb.at[1], emb_send.at[1], emb_recv.at[1], g, sibling)
    send_on = remote(emb.at[2], emb.at[3], emb_send.at[2], emb_recv.at[2], g, sibling)
    send_across.start()
    send_sibling.start()

    def tell(sem, grp):
        pl.semaphore_signal(sem, inc=1, device_id=(grp, s), device_id_type=MESH)

    tell(past, (g + 12) % 16)

    @pl.when(core == 1)
    def _():
        each(1, 4, lambda k: tell(past, zh * 4 + (y + k) % 4))


    def w1_copy(k):
        return remote(my_part, my_part, w1_send.at[k], w1_recv.at[zh], (g + 4 * k) % 16, s)

    @pl.when(x < 3)
    def _():
        load_wout.wait()
        w1_copy(1).start()
        w1_copy(3).start()

    def other_rows(slot):
        for j in range(6):
            cols = slice(256 * j, 256 * j + 256)
            kv_all[ROWS * slot : ROWS * slot + ROWS, cols] = dot(
                emb[slot], wq[:, WIDTH + 256 * j : WIDTH + 256 * j + 256]
            ).astype(BF16)

    send_sibling.wait_recv()
    other_rows(1)

    @pl.when(core == 1)
    def _():
        pl.semaphore_wait(past, 4)
        each(1, 4, lambda k: tell(past_too, zh * 4 + (y + k) % 4))

    @pl.when(core == 0)
    def _():
        pl.semaphore_wait(past, 1)

    @pl.when(x < 3)
    def _():
        w1_copy(2).start()

    e_own = chip // 8
    relay = remote(recv_a, recv_a, relay_send, relay_recv, g, sibling)
    give = remote(out2, out2, o2_send, o2_recv, g, sibling)

    def kv3_copy(k):
        block = kv3.at[y]
        return remote(block, block, kv3_send.at[k], kv3_recv.at[y], zh * 4 + (y + k) % 4, s)

    def far_copy(k):
        return remote(
            kv3.at[y, pl.ds(0, 32)], far.at[g], far_send.at[k], far_recv.at[g],
            ((zh + far_step(k)) % 4) * 4 + (y + 2 + k) % 4, s,
        )

    def far_step(k):
        return (k // 4) % 3 + 1

    @pl.when(core == 1)
    def _():
        pltpu.make_async_copy(recv_a, recv_a, a_recv).wait()
        relay.start()
        spot = iota((128, 512), 0)
        col = iota((128, 512), 1)
        pick = ((spot % 32) * 16 + 4 * e_own + spot // 32 == col).astype(F32).astype(BF16)
        chosen = dot(pick, recv_a[...].reshape(512, 256)).astype(BF16)
        kv3[y] = chosen[:, 0:128]
        q3[...] = chosen[:, 128:256]
        pl.semaphore_wait(past_too, 3)
        each(4, 16, lambda k: far_copy(k).start())
        each(1, 4, lambda k: kv3_copy(k).start())

    @pl.when(core == 0)
    def _():
        relay.wait_recv()

        def block(i, carry):
            rows = pl.ds(pl.multiple_of(128 * i, 128), 128)
            flat = recv_a[...].reshape(512, 256)
            queries = recv_a[pl.ds(8 * i, 8)][:, :, 128:256].reshape(128, 128)
            mixed, level = attend(queries, flat[:, 0:128])
            out2[rows, :] = jnp.where(lane128 < 48, level, mixed)
            return carry

        lax.fori_loop(0, 4, block, 0)
        give.start()

    send_across.wait_recv()
    send_on.start()
    other_rows(2)
    send_on.wait_recv()
    other_rows(3)

    def first_branch(rho, carry):
        b = (rho + 5) // 8
        off = 48 * rho - 128 * b
        lane = iota((1, 256), 1)
        mine = (lane >= off) & (lane < off + 48)
        keep = mine.astype(F32).astype(BF16)
        for e in range(2):
            w0 = 384 * e + 128 * b
            win = pl.ds(pl.multiple_of(w0, 128), 256)
            win_v = pl.ds(pl.multiple_of(WIDTH + w0, 128), 256)
            top, weights = soft(dot_nt(q_own[:, win] * keep, kv_all[:, win]))
            total = jnp.sum(weights, axis=1, keepdims=True)
            mixed = dot(weights.astype(BF16), kv_all[:, win_v]) * (1.0 / total)
            att[:, win] = jnp.where(mine, mixed, att[:, win])
            lse[rho + 8 * e] = jnp.broadcast_to(top * SCALE + jnp.log2(total), (ROWS, 128))
        return carry

    lax.fori_loop(0, 4, first_branch, 0)

    @pl.when(x < 3)
    def _():
        each(1, 4, lambda k: pltpu.make_async_copy(my_part, my_part, w1_recv.at[(zh + k) % 4]).wait())

    my_column = wall.at[:, y, x % 3, :, half_cols]

    def w2_copy(k):
        return remote(
            my_column, my_column, w2_send.at[k], w2_recv.at[(x % 3) * 4 + y],
            zh * 4 + (y + k % 4) % 4, ((x + k // 4) % 4) * 8 + s % 8,
        )

    @pl.when(x < 3)
    def _():
        each(1, 16, lambda k: w2_copy(k).start())

    def c_copy(k):
        there = 2 * seat(k // 2) + 1 - k % 2
        return remote(msg_c.at[there], recv_c.at[chip], c_send.at[k], c_recv, g, there)

    def c_all(act):
        each(0, 16, lambda k: act(c_copy(k)))
        each(17, 32, lambda k: act(c_copy(k)))

    @pl.when(core == 1)
    def _():
        each(1, 4, lambda k: pltpu.make_async_copy(kv3.at[0], kv3.at[0], kv3_recv.at[(y + k) % 4]).wait())
        mixed3, level3 = attend(q3[...], kv3[...].reshape(512, 128))
        give.wait_recv()

        def fold(m, a, l):
            rows = pl.ds(4 * e_own + m, 32, stride=16)
            held = out2[rows, :]
            a, l = merge(held, held[:, 0:1], a, l)
            out2[rows, :] = jnp.where(lane128 < 48, l, a)

        for m in range(4):
            fold(m, mixed3[32 * m : 32 * m + 32], level3[32 * m : 32 * m + 32])
        for k in range(4):
            far[zh * 4 + k] = kv3[k, 0:32, :]
        each(4, 16, lambda k: pltpu.make_async_copy(
            far.at[0], far.at[0], far_recv.at[((zh + k // 4) % 4) * 4 + k % 4]).wait())
        mixed4, level4 = attend(q3[0:32, :], far[...].reshape(512, 128))
        fold(0, mixed4, level4)
        done = out2[...]
        level = done[:, 0:1]
        high = level.astype(BF16).astype(F32)
        mid = (level - high).astype(BF16).astype(F32)
        low = level - high - mid
        coded = jnp.where(lane128 == 0, high, jnp.where(lane128 == 1, mid, jnp.where(lane128 == 2, low, done)))
        msg_c[...] = coded.astype(BF16).reshape(32, 16, 128)
        c_all(lambda c: c.start())
        pltpu.make_async_copy(msg_c.at[s], recv_c.at[chip], c_recv).start()

    lax.fori_loop(4, 8, first_branch, 0)

    def w3_part(i):
        piece = wall.at[:, :, i, :, half_cols]
        return remote(piece, piece, w3_send.at[i], w3_recv.at[i], g, sibling)

    def w3_start(i):
        def from_plane(j):
            @pl.when((i != x) | (j != y))
            def _():
                pltpu.make_async_copy(my_column, my_column, w2_recv.at[i * 4 + j]).wait()

        each(0, 4, from_plane)
        w3_part(i).start()

    each(0, 3, w3_start)

    pltpu.make_async_copy(recv_c, recv_c, c_recv).wait()
    for rho in range(8):
        base = 128 * (rho >= 3)
        off = 48 * rho - base
        src_row = iota((128, 256), 0)
        dst_lane = iota((128, 256), 1)
        put_back = ((src_row - 48 + off == dst_lane) & (src_row >= 48) & (src_row < 96)).astype(F32).astype(BF16)
        add_up = (src_row < 3).astype(F32).astype(BF16)
        lane = iota((1, 256), 1)
        mine = (lane >= off) & (lane < off + 48)
        rows = slice(16 * rho, 16 * rho + 16)
        for e in range(2):
            h = rho + 8 * e
            w0 = 384 * e + base
            other = dot(recv_c[h], put_back)
            level = dot(recv_c[h], add_up)
            own_level = lse[h, rows, 0:1]
            held = att[rows, w0 : w0 + 256]
            share = 1.0 / (1.0 + jnp.exp2(own_level - level))
            att[rows, w0 : w0 + 256] = jnp.where(mine, held + (other - held) * share, held)

    back = (row_order(iota((ROWS, ROWS), 1)) == iota((ROWS, ROWS), 0)).astype(F32).astype(BF16)
    attended = dot(back, att[...].astype(BF16)).astype(BF16)
    each(0, 3, lambda i: w3_part(i).wait_recv())
    for j in range(3):
        cols = slice(256 * j, 256 * j + 256)
        out_ref[:, cols] = dot(attended, wall[:, :, :, :, cols].reshape(WIDTH, 256)).astype(BF16)

    send_across.wait_send()
    send_sibling.wait_send()
    send_on.wait_send()
    a_all(lambda c: c.wait_send())

    @pl.when(core == 0)
    def _():
        give.wait_send()

    @pl.when(core == 1)
    def _():
        relay.wait_send()
        each(1, 4, lambda k: kv3_copy(k).wait_send())
        each(4, 16, lambda k: far_copy(k).wait_send())
        c_all(lambda c: c.wait_send())

    @pl.when(x < 3)
    def _():
        each(1, 4, lambda k: w1_copy(k).wait_send())
        each(1, 16, lambda k: w2_copy(k).wait_send())

    each(0, 3, lambda i: w3_part(i).wait_send())


def shards(tokens, tile_pos, w_qkv, w_out):
    dma = pltpu.SemaphoreType.DMA
    in_hbm = pl.BlockSpec(memory_space=pltpu.HBM)
    return pl.pallas_call(
        kernel,
        out_shape=jax.ShapeDtypeStruct((ROWS, WIDTH), BF16),
        in_specs=[in_hbm] * 4,
        out_specs=pl.BlockSpec(memory_space=pltpu.VMEM),
        scratch_shapes=[
            pltpu.VMEM((ROWS, WIDTH), BF16),
            pltpu.VMEM((2, ROWS), jnp.int32),
            pltpu.VMEM((WIDTH, 3 * WIDTH), BF16),
            pltpu.VMEM((4, ROWS, WIDTH), BF16),
            pltpu.VMEM((ROWS, WIDTH), BF16),
            pltpu.VMEM((4 * ROWS, 2 * WIDTH), BF16),
            pltpu.VMEM((HEADS, 16, 256), BF16),
            pltpu.VMEM((32, 16, 256), BF16),
            pltpu.VMEM((4, 128, 128), BF16),
            pltpu.VMEM((16, 32, 128), BF16),
            pltpu.VMEM((128, 128), BF16),
            pltpu.VMEM((512, 128), F32),
            pltpu.VMEM((32, 16, 128), BF16),
            pltpu.VMEM((HEADS, 16, 128), BF16),
            pltpu.VMEM((ROWS, WIDTH), F32),
            pltpu.VMEM((HEADS, ROWS, 128), F32),
            pltpu.VMEM((4, 4, 3, 16, WIDTH), BF16),
            dma((6,)), dma((3,)), dma((3,)), dma((16,)), dma, dma, dma,
            dma((4,)), dma((4,)), dma((16,)), dma((16,)), dma, dma, dma((32,)), dma,
            dma((4,)), dma((4,)), dma((16,)), dma((12,)), dma((3,)), dma((3,)),
            pltpu.SemaphoreType.REGULAR, pltpu.SemaphoreType.REGULAR,
        ],
        compiler_params=pltpu.CompilerParams(
            collective_id=0, has_side_effects=True, vmem_limit_bytes=60 * 1024 * 1024
        ),
        name="dilated_attention",
    )(tokens, tile_pos, w_qkv, w_out)


def solution(mesh):
    placed = (P(("grp", "seq"), None), P(None, ("grp", "seq")), P(), P("grp", None))
    return jax.shard_map(
        shards, mesh=mesh, in_specs=placed, out_specs=P(("grp", "seq"), None), check_vma=False
    )
```

```python
import jax
import jax.numpy as jnp
import numpy as np
from jax import lax
from jax.experimental import pallas as pl
from jax.experimental.pallas import tpu as pltpu
from jax.sharding import PartitionSpec as P

MESH = pl.DeviceIdType.MESH
F32 = jnp.float32
BF16 = jnp.bfloat16
ROWS = 128
WIDTH = 768
HEADS = 16
LOG2E = 1.4426950408889634
SCALE = 48 ** (-0.5) * LOG2E


def iota(shape, axis):
    return lax.broadcasted_iota(jnp.int32, shape, axis)


def dot(a, b):
    return jnp.dot(a, b, preferred_element_type=F32)


def dot_nt(a, b):
    return lax.dot_general(a, b, (((1,), (1,)), ((), ())), preferred_element_type=F32)


def row_order(p):
    return p // 16 + 8 * ((p % 4) * 4 + (p % 16) // 4)


def omega(lane):
    j = lane % 192
    rate = jnp.ones(lane.shape, F32)
    for bit in range(8):
        rate = jnp.where((j // 2**bit) % 2 == 1, rate * float(10000.0 ** (-(2**bit) / 192)), rate)
    return rate


def sine(angle, quarter_turns):
    turns = jnp.floor(angle * (2.0 / np.pi) + 0.5)
    rest = ((angle - turns * 1.5703125) - turns * 4.837512969970703125e-4) - turns * 7.54978995489188216e-8
    quadrant = turns.astype(jnp.int32) + quarter_turns
    sq = rest * rest
    sin_part = rest + rest * sq * (-1.6666654611e-1 + sq * (8.3321608736e-3 - sq * 1.9515295891e-4))
    cos_part = 1.0 - 0.5 * sq + sq * sq * (
        4.166664568298827e-2 + sq * (-1.388731625493765e-3 + sq * 2.443315711809948e-5)
    )
    value = jnp.where((quadrant & 1) == 1, cos_part, sin_part)
    return jnp.where((quadrant & 2) == 2, -value, value)


def soft(scores):
    top = jnp.max(scores, axis=1, keepdims=True)
    return top, jnp.exp2((scores - top) * SCALE)


def merge(a, l, b, m):
    gap = m - l
    share = 1.0 / (1.0 + jnp.exp2(-gap))
    both = jnp.maximum(l, m) + jnp.log2(1.0 + jnp.exp2(-jnp.abs(gap)))
    return a + (b - a) * share, both


def attend(queries, keys_values):
    top, weights = soft(dot_nt(queries, keys_values))
    mixed = dot(weights.astype(BF16), keys_values)
    total = mixed[:, 96:97]
    return mixed * (1.0 / total), top * SCALE + jnp.log2(total)


def kernel(
    tok_hbm, pos_hbm, wqkv_hbm, wout_hbm, out_ref,
    tok, pos, wq, emb, q_own, kv_all, msg, recv_a, kv3, far, q3, out2, msg_c, recv_c,
    att, lse, wall,
    load_sem, emb_send, emb_recv, a_send, a_recv, relay_send, relay_recv,
    kv3_send, kv3_recv, far_send, far_recv, o2_send, o2_recv, c_send, c_recv,
    w1_send, w1_recv, w2_send, w2_recv, w3_send, w3_recv, past, past_too,
):
    g = lax.axis_index("grp")
    s = lax.axis_index("seq")
    core = s % 2
    chip = s // 2
    x = s // 8
    zh = g // 4
    y = g % 4
    sibling = s + 1 - 2 * core
    across = s + 2 - 4 * (chip % 2)
    sender = (core == 0) & (x < 3)

    def remote(src, dst, send_sem, recv_sem, grp, seq):
        return pltpu.make_async_remote_copy(
            src_ref=src, dst_ref=dst, send_sem=send_sem, recv_sem=recv_sem,
            device_id=(grp, seq), device_id_type=MESH,
        )

    def each(low, high, body):
        def step(i, carry):
            body(i)
            return carry
        lax.fori_loop(low, high, step, 0)

    def seat(k):
        return ((x + 2 + k // 4) % 4) * 4 + (chip + k) % 4

    load_tok = pltpu.make_async_copy(tok_hbm, tok, load_sem.at[0])
    load_pos = pltpu.make_async_copy(pos_hbm, pos, load_sem.at[1])
    load_wq = [
        pltpu.make_async_copy(
            wqkv_hbm.at[:, pl.ds(WIDTH * i, WIDTH)], wq.at[:, pl.ds(WIDTH * i, WIDTH)], load_sem.at[2 + i]
        )
        for i in range(3)
    ]
    load_tok.start()
    load_pos.start()
    for item in load_wq:
        item.start()

    my_block = (zh * 4 + y) * 3 + x % 3
    load_wout = pltpu.make_async_copy(
        wout_hbm.at[pl.ds(pl.multiple_of(16 * (x % 3), 16), 16)], wall.at[my_block], load_sem.at[5]
    )

    @pl.when(sender)
    def _():
        load_wout.start()

    barrier = pltpu.get_barrier_semaphore()

    def greet(grp, seq):
        pl.semaphore_signal(barrier, inc=1, device_id=(grp, seq), device_id_type=MESH)

    @pl.when(core == 1)
    def _():
        greet((g + 4) % 16, s)
        greet((g + 12) % 16, s)
        each(1, 32, lambda k: greet(g, (s + k) % 32))
        each(1, 4, lambda k: greet(zh * 4 + (y + k) % 4, s))

    @pl.when(core == 0)
    def _():
        greet((g + 4) % 16, s)
        greet((g + 12) % 16, s)
        each(0, 16, lambda k: greet(g, 2 * k + 1))
        greet(g, across)
        each(1, 16, lambda k: greet(zh * 4 + (y + k % 4) % 4, ((x + k // 4) % 4) * 8 + s % 8))

    load_tok.wait()
    load_pos.wait()
    order = (row_order(iota((ROWS, ROWS), 0)) == iota((ROWS, ROWS), 1)).astype(F32)
    place = pos[...].astype(F32)
    pos_x = jnp.sum(order * place[0:1, :], axis=1, keepdims=True)
    pos_y = jnp.sum(order * place[1:2, :], axis=1, keepdims=True)
    order_bf = order.astype(BF16)
    for i in range(6):
        cols = slice(128 * i, 128 * i + 128)
        lane = iota((1, 128), 1) + 128 * i
        spot = pos_x if i < 3 else pos_y
        turn = ((lane % 384) >= 192).astype(jnp.int32)
        value = sine(spot * omega(lane), turn)
        emb[0, :, cols] = (dot(order_bf, tok[:, cols]) + value).astype(BF16)

    for i in range(3):
        load_wq[i].wait()
        for j in range(3):
            part = dot(emb[0], wq[:, WIDTH * i + 256 * j : WIDTH * i + 256 * j + 256]).astype(BF16)
            if i == 0:
                q_own[:, 256 * j : 256 * j + 256] = part
            else:
                first = WIDTH * (i - 1) + 256 * j
                kv_all[0:ROWS, first : first + 256] = part

    lane128 = iota((1, 128), 1)
    for rho in range(8):
        base = 128 * (rho >= 3)
        off = 48 * rho - base
        src_row = iota((256, 128), 0)
        dst_lane = iota((256, 128), 1)
        put_first = ((src_row == dst_lane + off) & (dst_lane < 48)).astype(F32).astype(BF16)
        put_second = (
            (src_row == dst_lane - 48 + off) & (dst_lane >= 48) & (dst_lane < 96)
        ).astype(F32).astype(BF16)
        rows = slice(16 * rho, 16 * rho + 16)
        for e in range(2):
            h = rho + 8 * e
            w0 = 384 * e + base
            q_part = dot(q_own[rows, w0 : w0 + 256], put_first)
            kv_part = dot(kv_all[rows, w0 : w0 + 256], put_first) + dot(
                kv_all[rows, WIDTH + w0 : WIDTH + w0 + 256], put_second
            )
            kv_part = jnp.where(lane128 >= 96, 1.0, kv_part)
            msg[h, :, 0:128] = kv_part.astype(BF16)
            msg[h, :, 128:256] = q_part.astype(BF16)

    @pl.when(core == 1)
    def _():
        pl.semaphore_wait(barrier, 36)

    @pl.when(core == 0)
    def _():
        pl.semaphore_wait(barrier, 34)

    def a_copy(k):
        h = seat(k)
        return remote(msg.at[h], recv_a.at[s], a_send.at[k], a_recv, g, 2 * h + 1)

    a_local = pltpu.make_async_copy(msg.at[chip], recv_a.at[s], a_recv)

    def a_all(act):
        each(0, 8, lambda k: act(a_copy(k)))
        each(9, 16, lambda k: act(a_copy(k)))

        @pl.when(core == 0)
        def _():
            act(a_copy(8))

    a_all(lambda c: c.start())

    @pl.when(core == 1)
    def _():
        a_local.start()

    send_across = remote(emb.at[0], emb.at[2], emb_send.at[0], emb_recv.at[0], g, across)
    send_sibling = remote(emb.at[0], emb.at[1], emb_send.at[1], emb_recv.at[1], g, sibling)
    send_on = remote(emb.at[2], emb.at[3], emb_send.at[2], emb_recv.at[2], g, sibling)
    send_across.start()
    send_sibling.start()

    def tell(sem, grp):
        pl.semaphore_signal(sem, inc=1, device_id=(grp, s), device_id_type=MESH)

    @pl.when(core == 1)
    def _():
        tell(past, (g + 12) % 16)
        each(1, 4, lambda k: tell(past, zh * 4 + (y + k) % 4))

    def block_of(step):
        return (((zh + step) % 4) * 4 + y) * 3 + x % 3

    def w1_copy(k, step):
        block = wall.at[block_of(step)]
        return remote(
            block, block, w1_send.at[k + step], w1_recv.at[(zh + step) % 4], (g + 4 * k + 16) % 16, s
        )

    def w1_wait(step):
        block = wall.at[block_of(step)]
        pltpu.make_async_copy(block, block, w1_recv.at[(zh + step) % 4]).wait()

    def w2_copy(k, step):
        block = wall.at[block_of(step)]
        return remote(
            block, block, w2_send.at[step, k], w2_recv.at[(zh + step) % 4],
            zh * 4 + (y + k % 4) % 4, ((x + k // 4) % 4) * 8 + s % 8,
        )

    def w2_start(step):
        each(1, 16, lambda k: w2_copy(k, step).start())

    def w2_wait(step):
        sem = w2_recv.at[(zh + step) % 4]

        @pl.when(x < 3)
        def _():
            pltpu.make_async_copy(wall.at[pl.ds(0, 11)], wall.at[pl.ds(0, 11)], sem).wait()

        @pl.when(x == 3)
        def _():
            pltpu.make_async_copy(wall.at[pl.ds(0, 12)], wall.at[pl.ds(0, 12)], sem).wait()

    def w3_copy(i):
        blocks = wall.at[pl.ds(12 * i, 12)]
        return remote(blocks, blocks, w3_send.at[i], w3_recv.at[i], g, sibling)

    def w3_start(step):
        w2_wait(step)
        w3_copy((zh + step) % 4).start()

    @pl.when(sender)
    def _():
        load_wout.wait()
        w1_copy(1, 0).start()
        w1_copy(3, 0).start()
        w2_start(0)

    def other_rows(slot):
        for j in range(6):
            cols = slice(256 * j, 256 * j + 256)
            kv_all[ROWS * slot : ROWS * slot + ROWS, cols] = dot(
                emb[slot], wq[:, WIDTH + 256 * j : WIDTH + 256 * j + 256]
            ).astype(BF16)

    send_sibling.wait_recv()
    other_rows(1)

    @pl.when(core == 1)
    def _():
        pl.semaphore_wait(past, 4)
        each(1, 4, lambda k: tell(past_too, zh * 4 + (y + k) % 4))

    @pl.when(sender)
    def _():
        w1_wait(1)
        w1_copy(3, 1).start()
        w1_wait(3)
        w2_start(1)
        w2_start(3)

    e_own = chip // 8
    relay = remote(recv_a, recv_a, relay_send, relay_recv, g, sibling)
    give = remote(out2, out2, o2_send, o2_recv, g, sibling)

    def kv3_copy(k):
        block = kv3.at[y]
        return remote(block, block, kv3_send.at[k], kv3_recv.at[y], zh * 4 + (y + k) % 4, s)

    def far_copy(k):
        return remote(
            kv3.at[y, pl.ds(0, 32)], far.at[g], far_send.at[k], far_recv.at[g],
            ((zh + far_step(k)) % 4) * 4 + (y + 2 + k) % 4, s,
        )

    def far_step(k):
        return (k // 4) % 3 + 1

    @pl.when(core == 1)
    def _():
        pltpu.make_async_copy(recv_a, recv_a, a_recv).wait()
        relay.start()
        spot = iota((128, 512), 0)
        col = iota((128, 512), 1)
        pick = ((spot % 32) * 16 + 4 * e_own + spot // 32 == col).astype(F32).astype(BF16)
        chosen = dot(pick, recv_a[...].reshape(512, 256)).astype(BF16)
        kv3[y] = chosen[:, 0:128]
        q3[...] = chosen[:, 128:256]
        pl.semaphore_wait(past_too, 3)
        each(4, 16, lambda k: far_copy(k).start())
        each(1, 4, lambda k: kv3_copy(k).start())

    @pl.when(core == 0)
    def _():
        relay.wait_recv()

        def block(i, carry):
            rows = pl.ds(pl.multiple_of(128 * i, 128), 128)
            flat = recv_a[...].reshape(512, 256)
            queries = recv_a[pl.ds(8 * i, 8)][:, :, 128:256].reshape(128, 128)
            mixed, level = attend(queries, flat[:, 0:128])
            out2[rows, :] = jnp.where(lane128 < 48, level, mixed)
            return carry

        lax.fori_loop(0, 4, block, 0)
        give.start()

    @pl.when(sender)
    def _():
        w1_wait(2)
        w2_start(2)

    send_across.wait_recv()
    send_on.start()
    other_rows(2)
    send_on.wait_recv()
    other_rows(3)

    def first_branch(rho, carry):
        b = (rho + 5) // 8
        off = 48 * rho - 128 * b
        lane = iota((1, 256), 1)
        mine = (lane >= off) & (lane < off + 48)
        keep = mine.astype(F32).astype(BF16)
        for e in range(2):
            w0 = 384 * e + 128 * b
            win = pl.ds(pl.multiple_of(w0, 128), 256)
            win_v = pl.ds(pl.multiple_of(WIDTH + w0, 128), 256)
            top, weights = soft(dot_nt(q_own[:, win] * keep, kv_all[:, win]))
            total = jnp.sum(weights, axis=1, keepdims=True)
            mixed = dot(weights.astype(BF16), kv_all[:, win_v]) * (1.0 / total)
            att[:, win] = jnp.where(mine, mixed, att[:, win])
            lse[rho + 8 * e] = jnp.broadcast_to(top * SCALE + jnp.log2(total), (ROWS, 128))
        return carry

    lax.fori_loop(0, 4, first_branch, 0)

    @pl.when(core == 0)
    def _():
        w3_start(0)
        w3_start(1)
        w3_start(3)

    def c_copy(k):
        there = 2 * seat(k // 2) + 1 - k % 2
        return remote(msg_c.at[there], recv_c.at[chip], c_send.at[k], c_recv, g, there)

    def c_all(act):
        each(0, 16, lambda k: act(c_copy(k)))
        each(17, 32, lambda k: act(c_copy(k)))

    @pl.when(core == 1)
    def _():
        each(1, 4, lambda k: pltpu.make_async_copy(kv3.at[0], kv3.at[0], kv3_recv.at[(y + k) % 4]).wait())
        mixed3, level3 = attend(q3[...], kv3[...].reshape(512, 128))
        give.wait_recv()

        def fold(m, a, l):
            rows = pl.ds(4 * e_own + m, 32, stride=16)
            held = out2[rows, :]
            a, l = merge(held, held[:, 0:1], a, l)
            out2[rows, :] = jnp.where(lane128 < 48, l, a)

        for m in range(4):
            fold(m, mixed3[32 * m : 32 * m + 32], level3[32 * m : 32 * m + 32])
        for k in range(4):
            far[zh * 4 + k] = kv3[k, 0:32, :]
        each(4, 16, lambda k: pltpu.make_async_copy(
            far.at[0], far.at[0], far_recv.at[((zh + k // 4) % 4) * 4 + k % 4]).wait())
        mixed4, level4 = attend(q3[0:32, :], far[...].reshape(512, 128))
        fold(0, mixed4, level4)
        done = out2[...]
        level = done[:, 0:1]
        high = level.astype(BF16).astype(F32)
        mid = (level - high).astype(BF16).astype(F32)
        low = level - high - mid
        coded = jnp.where(lane128 == 0, high, jnp.where(lane128 == 1, mid, jnp.where(lane128 == 2, low, done)))
        msg_c[...] = coded.astype(BF16).reshape(32, 16, 128)
        c_all(lambda c: c.start())
        pltpu.make_async_copy(msg_c.at[s], recv_c.at[chip], c_recv).start()

    lax.fori_loop(4, 8, first_branch, 0)

    @pl.when(core == 0)
    def _():
        w3_start(2)

    pltpu.make_async_copy(recv_c, recv_c, c_recv).wait()
    for rho in range(8):
        base = 128 * (rho >= 3)
        off = 48 * rho - base
        src_row = iota((128, 256), 0)
        dst_lane = iota((128, 256), 1)
        put_back = ((src_row - 48 + off == dst_lane) & (src_row >= 48) & (src_row < 96)).astype(F32).astype(BF16)
        add_up = (src_row < 3).astype(F32).astype(BF16)
        lane = iota((1, 256), 1)
        mine = (lane >= off) & (lane < off + 48)
        rows = slice(16 * rho, 16 * rho + 16)
        for e in range(2):
            h = rho + 8 * e
            w0 = 384 * e + base
            other = dot(recv_c[h], put_back)
            level = dot(recv_c[h], add_up)
            own_level = lse[h, rows, 0:1]
            held = att[rows, w0 : w0 + 256]
            share = 1.0 / (1.0 + jnp.exp2(own_level - level))
            att[rows, w0 : w0 + 256] = jnp.where(mine, held + (other - held) * share, held)

    back = (row_order(iota((ROWS, ROWS), 1)) == iota((ROWS, ROWS), 0)).astype(F32).astype(BF16)
    attended = dot(back, att[...].astype(BF16)).astype(BF16)

    @pl.when(core == 1)
    def _():
        each(0, 4, lambda i: w3_copy(i).wait_recv())

    for j in range(3):
        cols = slice(256 * j, 256 * j + 256)
        out_ref[:, cols] = dot(attended, wall[:, :, cols].reshape(WIDTH, 256)).astype(BF16)

    send_across.wait_send()
    send_sibling.wait_send()
    send_on.wait_send()
    a_all(lambda c: c.wait_send())

    @pl.when(core == 0)
    def _():
        give.wait_send()

    @pl.when(core == 1)
    def _():
        relay.wait_send()
        each(1, 4, lambda k: kv3_copy(k).wait_send())
        each(4, 16, lambda k: far_copy(k).wait_send())
        c_all(lambda c: c.wait_send())

    @pl.when(core == 0)
    def _():
        each(0, 4, lambda i: w3_copy(i).wait_send())

    @pl.when(sender)
    def _():
        w1_copy(1, 0).wait_send()
        w1_copy(3, 0).wait_send()
        w1_copy(3, 1).wait_send()
        for step in range(4):
            each(1, 16, lambda k, step=step: w2_copy(k, step).wait_send())


def shards(tokens, tile_pos, w_qkv, w_out):
    dma = pltpu.SemaphoreType.DMA
    in_hbm = pl.BlockSpec(memory_space=pltpu.HBM)
    return pl.pallas_call(
        kernel,
        out_shape=jax.ShapeDtypeStruct((ROWS, WIDTH), BF16),
        in_specs=[in_hbm] * 4,
        out_specs=pl.BlockSpec(memory_space=pltpu.VMEM),
        scratch_shapes=[
            pltpu.VMEM((ROWS, WIDTH), BF16),
            pltpu.VMEM((2, ROWS), jnp.int32),
            pltpu.VMEM((WIDTH, 3 * WIDTH), BF16),
            pltpu.VMEM((4, ROWS, WIDTH), BF16),
            pltpu.VMEM((ROWS, WIDTH), BF16),
            pltpu.VMEM((4 * ROWS, 2 * WIDTH), BF16),
            pltpu.VMEM((HEADS, 16, 256), BF16),
            pltpu.VMEM((32, 16, 256), BF16),
            pltpu.VMEM((4, 128, 128), BF16),
            pltpu.VMEM((16, 32, 128), BF16),
            pltpu.VMEM((128, 128), BF16),
            pltpu.VMEM((512, 128), F32),
            pltpu.VMEM((32, 16, 128), BF16),
            pltpu.VMEM((HEADS, 16, 128), BF16),
            pltpu.VMEM((ROWS, WIDTH), F32),
            pltpu.VMEM((HEADS, ROWS, 128), F32),
            pltpu.VMEM((48, 16, WIDTH), BF16),
            dma((6,)), dma((3,)), dma((3,)), dma((16,)), dma, dma, dma,
            dma((4,)), dma((4,)), dma((16,)), dma((16,)), dma, dma, dma((32,)), dma,
            dma((5,)), dma((4,)), dma((4, 16)), dma((4,)), dma((4,)), dma((4,)),
            pltpu.SemaphoreType.REGULAR, pltpu.SemaphoreType.REGULAR,
        ],
        compiler_params=pltpu.CompilerParams(
            collective_id=0, has_side_effects=True, vmem_limit_bytes=60 * 1024 * 1024
        ),
        name="dilated_attention",
    )(tokens, tile_pos, w_qkv, w_out)


def solution(mesh):
    placed = (P(("grp", "seq"), None), P(None, ("grp", "seq")), P(), P("grp", None))
    return jax.shard_map(
        shards, mesh=mesh, in_specs=placed, out_specs=P(("grp", "seq"), None), check_vma=False
    )
```

```python
import jax
import jax.numpy as jnp
import numpy as np
from jax import lax
from jax.experimental import pallas as pl
from jax.experimental.pallas import tpu as pltpu
from jax.sharding import PartitionSpec as P

MESH = pl.DeviceIdType.MESH
F32 = jnp.float32
BF16 = jnp.bfloat16
ROWS = 128
WIDTH = 768
HEADS = 16
LOG2E = 1.4426950408889634
SCALE = 48 ** (-0.5) * LOG2E


def iota(shape, axis):
    return lax.broadcasted_iota(jnp.int32, shape, axis)


def dot(a, b):
    return jnp.dot(a, b, preferred_element_type=F32)


def dot_nt(a, b):
    return lax.dot_general(a, b, (((1,), (1,)), ((), ())), preferred_element_type=F32)


def row_order(p):
    return p // 16 + 8 * ((p % 4) * 4 + (p % 16) // 4)


def omega(lane):
    j = lane % 192
    rate = jnp.ones(lane.shape, F32)
    for bit in range(8):
        rate = jnp.where((j // 2**bit) % 2 == 1, rate * float(10000.0 ** (-(2**bit) / 192)), rate)
    return rate


def sine(angle, quarter_turns):
    turns = jnp.floor(angle * (2.0 / np.pi) + 0.5)
    rest = ((angle - turns * 1.5703125) - turns * 4.837512969970703125e-4) - turns * 7.54978995489188216e-8
    quadrant = turns.astype(jnp.int32) + quarter_turns
    sq = rest * rest
    sin_part = rest + rest * sq * (-1.6666654611e-1 + sq * (8.3321608736e-3 - sq * 1.9515295891e-4))
    cos_part = 1.0 - 0.5 * sq + sq * sq * (
        4.166664568298827e-2 + sq * (-1.388731625493765e-3 + sq * 2.443315711809948e-5)
    )
    value = jnp.where((quadrant & 1) == 1, cos_part, sin_part)
    return jnp.where((quadrant & 2) == 2, -value, value)


def soft(scores):
    top = jnp.max(scores, axis=1, keepdims=True)
    return top, jnp.exp2((scores - top) * SCALE)


def merge(a, l, b, m):
    gap = m - l
    share = 1.0 / (1.0 + jnp.exp2(-gap))
    both = jnp.maximum(l, m) + jnp.log2(1.0 + jnp.exp2(-jnp.abs(gap)))
    return a + (b - a) * share, both


def attend(queries, keys_values):
    top, weights = soft(dot_nt(queries, keys_values))
    mixed = dot(weights.astype(BF16), keys_values)
    total = mixed[:, 96:97]
    return mixed * (1.0 / total), top * SCALE + jnp.log2(total)


def kernel(
    tok_hbm, pos_hbm, wqkv_hbm, wout_hbm, out_ref,
    tok, pos, wq, emb, q_own, kv_all, msg, recv_a, kv3, far, q3, out2, msg_c, recv_c,
    att, lse, wall,
    load_sem, emb_send, emb_recv, a_send, a_recv, relay_send, relay_recv,
    kv3_send, kv3_recv, far_send, far_recv, o2_send, o2_recv, c_send, c_recv,
    w1_send, w1_recv, wx_send, wx_recv, wy_send, wy_recv, wf_send, wf_recv, w3_send, w3_recv, past, past_too,
):
    g = lax.axis_index("grp")
    s = lax.axis_index("seq")
    core = s % 2
    chip = s // 2
    x = s // 8
    zh = g // 4
    y = g % 4
    sibling = s + 1 - 2 * core
    across = s + 2 - 4 * (chip % 2)

    def remote(src, dst, send_sem, recv_sem, grp, seq):
        return pltpu.make_async_remote_copy(
            src_ref=src, dst_ref=dst, send_sem=send_sem, recv_sem=recv_sem,
            device_id=(grp, seq), device_id_type=MESH,
        )

    def each(low, high, body):
        def step(i, carry):
            body(i)
            return carry
        lax.fori_loop(low, high, step, 0)

    def seat(k):
        return ((x + 2 + k // 4) % 4) * 4 + (chip + k) % 4

    load_tok = pltpu.make_async_copy(tok_hbm, tok, load_sem.at[0])
    load_pos = pltpu.make_async_copy(pos_hbm, pos, load_sem.at[1])
    load_wq = [
        pltpu.make_async_copy(
            wqkv_hbm.at[:, pl.ds(WIDTH * i, WIDTH)], wq.at[:, pl.ds(WIDTH * i, WIDTH)], load_sem.at[2 + i]
        )
        for i in range(3)
    ]
    load_tok.start()
    load_pos.start()
    for item in load_wq:
        item.start()

    def part_at(step):
        return (x - zh - step + 8) % 4

    def block_at(step, off):
        return (((zh + step) % 4) * 4 + (y + off + 4) % 4) * 3

    load_wout = pltpu.make_async_copy(
        wout_hbm.at[pl.ds(pl.multiple_of(16 * (part_at(0) % 3), 16), 16)],
        wall.at[block_at(0, 0) + part_at(0) % 3], load_sem.at[5],
    )

    def bringing(step, act):
        pl.when((core == 0) & (part_at(step) < 3))(act)

    bringing(0, load_wout.start)

    barrier = pltpu.get_barrier_semaphore()

    def greet(grp, seq):
        pl.semaphore_signal(barrier, inc=1, device_id=(grp, seq), device_id_type=MESH)

    @pl.when(core == 1)
    def _():
        greet((g + 4) % 16, s)
        greet((g + 12) % 16, s)
        each(1, 32, lambda k: greet(g, (s + k) % 32))
        each(1, 4, lambda k: greet(zh * 4 + (y + k) % 4, s))

    @pl.when(core == 0)
    def _():
        greet((g + 4) % 16, s)
        greet((g + 12) % 16, s)
        each(0, 16, lambda k: greet(g, 2 * k + 1))
        greet(g, across)
        each(1, 4, lambda k: greet(g, ((x + k) % 4) * 8 + s % 8))
        greet(zh * 4 + (y + 1) % 4, s)
        greet(zh * 4 + (y + 3) % 4, s)

    load_tok.wait()
    load_pos.wait()
    order = (row_order(iota((ROWS, ROWS), 0)) == iota((ROWS, ROWS), 1)).astype(F32)
    place = pos[...].astype(F32)
    pos_x = jnp.sum(order * place[0:1, :], axis=1, keepdims=True)
    pos_y = jnp.sum(order * place[1:2, :], axis=1, keepdims=True)
    order_bf = order.astype(BF16)
    for i in range(6):
        cols = slice(128 * i, 128 * i + 128)
        lane = iota((1, 128), 1) + 128 * i
        spot = pos_x if i < 3 else pos_y
        turn = ((lane % 384) >= 192).astype(jnp.int32)
        value = sine(spot * omega(lane), turn)
        emb[0, :, cols] = (dot(order_bf, tok[:, cols]) + value).astype(BF16)

    for i in range(3):
        load_wq[i].wait()
        for j in range(3):
            part = dot(emb[0], wq[:, WIDTH * i + 256 * j : WIDTH * i + 256 * j + 256]).astype(BF16)
            if i == 0:
                q_own[:, 256 * j : 256 * j + 256] = part
            else:
                first = WIDTH * (i - 1) + 256 * j
                kv_all[0:ROWS, first : first + 256] = part

    lane128 = iota((1, 128), 1)
    for rho in range(8):
        base = 128 * (rho >= 3)
        off = 48 * rho - base
        src_row = iota((256, 128), 0)
        dst_lane = iota((256, 128), 1)
        put_first = ((src_row == dst_lane + off) & (dst_lane < 48)).astype(F32).astype(BF16)
        put_second = (
            (src_row == dst_lane - 48 + off) & (dst_lane >= 48) & (dst_lane < 96)
        ).astype(F32).astype(BF16)
        rows = slice(16 * rho, 16 * rho + 16)
        for e in range(2):
            h = rho + 8 * e
            w0 = 384 * e + base
            q_part = dot(q_own[rows, w0 : w0 + 256], put_first)
            kv_part = dot(kv_all[rows, w0 : w0 + 256], put_first) + dot(
                kv_all[rows, WIDTH + w0 : WIDTH + w0 + 256], put_second
            )
            kv_part = jnp.where(lane128 >= 96, 1.0, kv_part)
            msg[h, :, 0:128] = kv_part.astype(BF16)
            msg[h, :, 128:256] = q_part.astype(BF16)

    @pl.when(core == 1)
    def _():
        pl.semaphore_wait(barrier, 36)

    @pl.when(core == 0)
    def _():
        pl.semaphore_wait(barrier, 24)

    def a_copy(k):
        h = seat(k)
        return remote(msg.at[h], recv_a.at[s], a_send.at[k], a_recv, g, 2 * h + 1)

    a_local = pltpu.make_async_copy(msg.at[chip], recv_a.at[s], a_recv)

    def a_all(act):
        each(0, 8, lambda k: act(a_copy(k)))
        each(9, 16, lambda k: act(a_copy(k)))

        @pl.when(core == 0)
        def _():
            act(a_copy(8))

    a_all(lambda c: c.start())

    @pl.when(core == 1)
    def _():
        a_local.start()

    send_across = remote(emb.at[0], emb.at[2], emb_send.at[0], emb_recv.at[0], g, across)
    send_sibling = remote(emb.at[0], emb.at[1], emb_send.at[1], emb_recv.at[1], g, sibling)
    send_on = remote(emb.at[2], emb.at[3], emb_send.at[2], emb_recv.at[2], g, sibling)
    send_across.start()
    send_sibling.start()

    def tell(sem, grp):
        pl.semaphore_signal(sem, inc=1, device_id=(grp, s), device_id_type=MESH)

    @pl.when(core == 1)
    def _():
        tell(past, (g + 12) % 16)
        each(1, 4, lambda k: tell(past, zh * 4 + (y + k) % 4))

    def w1_copy(k, step):
        block = wall.at[block_at(step, 0) + part_at(step) % 3]
        return remote(
            block, block, w1_send.at[k + step], w1_recv.at[(zh + step) % 4], (g + 4 * k + 16) % 16, s
        )

    def w1_wait(step):
        block = wall.at[block_at(step, 0) + part_at(step) % 3]
        pltpu.make_async_copy(block, block, w1_recv.at[(zh + step) % 4]).wait()

    def wx_copy(step, k):
        block = wall.at[block_at(step, 0) + part_at(step) % 3]
        return remote(
            block, block, wx_send.at[step, k], wx_recv.at[(zh + step) % 4], g, ((x + k) % 4) * 8 + s % 8
        )

    def wy_copy(step, way):
        blocks = wall.at[pl.ds(block_at(step, 0), 3)]
        return remote(
            blocks, blocks, wy_send.at[step, way], wy_recv.at[(zh + step) % 4, way],
            zh * 4 + (y + 1 + 2 * way) % 4, s,
        )

    def wf_copy(step, way):
        blocks = wall.at[pl.ds(block_at(step, 2 * way - 1), 3), :, pl.ds(384 * way, 384)]
        return remote(
            blocks, blocks, wf_send.at[step, way], wf_recv.at[(zh + step) % 4, way],
            zh * 4 + (y + 1 + 2 * way) % 4, s,
        )

    def w3_copy(i):
        blocks = wall.at[pl.ds(12 * i, 12)]
        return remote(blocks, blocks, w3_send.at[i], w3_recv.at[i], g, sibling)

    def wx_start(step):
        def act():
            each(1, 4, lambda k: wx_copy(step, k).start())
        bringing(step, act)

    def wy_start(step):
        sem = wx_recv.at[(zh + step) % 4]

        @pl.when(part_at(step) < 3)
        def _():
            pltpu.make_async_copy(wall.at[pl.ds(0, 2)], wall.at[pl.ds(0, 2)], sem).wait()

        @pl.when(part_at(step) == 3)
        def _():
            pltpu.make_async_copy(wall.at[pl.ds(0, 3)], wall.at[pl.ds(0, 3)], sem).wait()

        wy_copy(step, 0).start()
        wy_copy(step, 1).start()

    def wf_start(step):
        for way in range(2):
            wy_copy(step, way).wait_recv()
            wf_copy(step, way).start()

    def w3_start(step):
        for way in range(2):
            wf_copy(step, way).wait_recv()
        w3_copy((zh + step) % 4).start()

    def first_w1():
        load_wout.wait()
        w1_copy(1, 0).start()
        w1_copy(3, 0).start()

    bringing(0, first_w1)
    wx_start(0)

    def other_rows(slot):
        for j in range(6):
            cols = slice(256 * j, 256 * j + 256)
            kv_all[ROWS * slot : ROWS * slot + ROWS, cols] = dot(
                emb[slot], wq[:, WIDTH + 256 * j : WIDTH + 256 * j + 256]
            ).astype(BF16)

    send_sibling.wait_recv()
    other_rows(1)

    @pl.when(core == 1)
    def _():
        pl.semaphore_wait(past, 4)
        each(1, 4, lambda k: tell(past_too, zh * 4 + (y + k) % 4))

    def pass_on():
        w1_wait(1)
        w1_copy(3, 1).start()

    @pl.when(core == 0)
    def _():
        wy_start(0)

    bringing(1, pass_on)
    wx_start(1)
    bringing(3, lambda: w1_wait(3))
    wx_start(3)

    @pl.when(core == 0)
    def _():
        wf_start(0)
        wy_start(1)
        wy_start(3)

    e_own = chip // 8
    relay = remote(recv_a, recv_a, relay_send, relay_recv, g, sibling)
    give = remote(out2, out2, o2_send, o2_recv, g, sibling)

    def kv3_copy(k):
        block = kv3.at[y]
        return remote(block, block, kv3_send.at[k], kv3_recv.at[y], zh * 4 + (y + k) % 4, s)

    def far_copy(k):
        return remote(
            kv3.at[y, pl.ds(0, 32)], far.at[g], far_send.at[k], far_recv.at[g],
            ((zh + far_step(k)) % 4) * 4 + (y + 2 + k) % 4, s,
        )

    def far_step(k):
        return (k // 4) % 3 + 1

    @pl.when(core == 1)
    def _():
        pltpu.make_async_copy(recv_a, recv_a, a_recv).wait()
        relay.start()
        spot = iota((128, 512), 0)
        col = iota((128, 512), 1)
        pick = ((spot % 32) * 16 + 4 * e_own + spot // 32 == col).astype(F32).astype(BF16)
        chosen = dot(pick, recv_a[...].reshape(512, 256)).astype(BF16)
        kv3[y] = chosen[:, 0:128]
        q3[...] = chosen[:, 128:256]
        pl.semaphore_wait(past_too, 3)
        each(4, 16, lambda k: far_copy(k).start())
        each(1, 4, lambda k: kv3_copy(k).start())

    @pl.when(core == 0)
    def _():
        relay.wait_recv()

        def block(i, carry):
            rows = pl.ds(pl.multiple_of(128 * i, 128), 128)
            flat = recv_a[...].reshape(512, 256)
            queries = recv_a[pl.ds(8 * i, 8)][:, :, 128:256].reshape(128, 128)
            mixed, level = attend(queries, flat[:, 0:128])
            out2[rows, :] = jnp.where(lane128 < 48, level, mixed)
            return carry

        lax.fori_loop(0, 4, block, 0)
        give.start()

    bringing(2, lambda: w1_wait(2))
    wx_start(2)

    @pl.when(core == 0)
    def _():
        wf_start(1)
        wf_start(3)
        w3_start(0)

    send_across.wait_recv()
    send_on.start()
    other_rows(2)
    send_on.wait_recv()
    other_rows(3)

    @pl.when(core == 0)
    def _():
        wy_start(2)
        w3_start(1)
        w3_start(3)

    def first_branch(rho, carry):
        b = (rho + 5) // 8
        off = 48 * rho - 128 * b
        lane = iota((1, 256), 1)
        mine = (lane >= off) & (lane < off + 48)
        keep = mine.astype(F32).astype(BF16)
        for e in range(2):
            w0 = 384 * e + 128 * b
            win = pl.ds(pl.multiple_of(w0, 128), 256)
            win_v = pl.ds(pl.multiple_of(WIDTH + w0, 128), 256)
            top, weights = soft(dot_nt(q_own[:, win] * keep, kv_all[:, win]))
            total = jnp.sum(weights, axis=1, keepdims=True)
            mixed = dot(weights.astype(BF16), kv_all[:, win_v]) * (1.0 / total)
            att[:, win] = jnp.where(mine, mixed, att[:, win])
            lse[rho + 8 * e] = jnp.broadcast_to(top * SCALE + jnp.log2(total), (ROWS, 128))
        return carry

    lax.fori_loop(0, 4, first_branch, 0)

    @pl.when(core == 0)
    def _():
        wf_start(2)

    def c_copy(k):
        there = 2 * seat(k // 2) + 1 - k % 2
        return remote(msg_c.at[there], recv_c.at[chip], c_send.at[k], c_recv, g, there)

    def c_all(act):
        each(0, 16, lambda k: act(c_copy(k)))
        each(17, 32, lambda k: act(c_copy(k)))

    @pl.when(core == 1)
    def _():
        each(1, 4, lambda k: pltpu.make_async_copy(kv3.at[0], kv3.at[0], kv3_recv.at[(y + k) % 4]).wait())
        mixed3, level3 = attend(q3[...], kv3[...].reshape(512, 128))
        give.wait_recv()

        def fold(m, a, l):
            rows = pl.ds(4 * e_own + m, 32, stride=16)
            held = out2[rows, :]
            a, l = merge(held, held[:, 0:1], a, l)
            out2[rows, :] = jnp.where(lane128 < 48, l, a)

        for m in range(4):
            fold(m, mixed3[32 * m : 32 * m + 32], level3[32 * m : 32 * m + 32])
        for k in range(4):
            far[zh * 4 + k] = kv3[k, 0:32, :]
        each(4, 16, lambda k: pltpu.make_async_copy(
            far.at[0], far.at[0], far_recv.at[((zh + k // 4) % 4) * 4 + k % 4]).wait())
        mixed4, level4 = attend(q3[0:32, :], far[...].reshape(512, 128))
        fold(0, mixed4, level4)
        done = out2[...]
        level = done[:, 0:1]
        high = level.astype(BF16).astype(F32)
        mid = (level - high).astype(BF16).astype(F32)
        low = level - high - mid
        coded = jnp.where(lane128 == 0, high, jnp.where(lane128 == 1, mid, jnp.where(lane128 == 2, low, done)))
        msg_c[...] = coded.astype(BF16).reshape(32, 16, 128)
        c_all(lambda c: c.start())
        pltpu.make_async_copy(msg_c.at[s], recv_c.at[chip], c_recv).start()

    lax.fori_loop(4, 8, first_branch, 0)

    @pl.when(core == 0)
    def _():
        w3_start(2)

    pltpu.make_async_copy(recv_c, recv_c, c_recv).wait()
    for rho in range(8):
        base = 128 * (rho >= 3)
        off = 48 * rho - base
        src_row = iota((128, 256), 0)
        dst_lane = iota((128, 256), 1)
        put_back = ((src_row - 48 + off == dst_lane) & (src_row >= 48) & (src_row < 96)).astype(F32).astype(BF16)
        add_up = (src_row < 3).astype(F32).astype(BF16)
        lane = iota((1, 256), 1)
        mine = (lane >= off) & (lane < off + 48)
        rows = slice(16 * rho, 16 * rho + 16)
        for e in range(2):
            h = rho + 8 * e
            w0 = 384 * e + base
            other = dot(recv_c[h], put_back)
            level = dot(recv_c[h], add_up)
            own_level = lse[h, rows, 0:1]
            held = att[rows, w0 : w0 + 256]
            share = 1.0 / (1.0 + jnp.exp2(own_level - level))
            att[rows, w0 : w0 + 256] = jnp.where(mine, held + (other - held) * share, held)

    back = (row_order(iota((ROWS, ROWS), 1)) == iota((ROWS, ROWS), 0)).astype(F32).astype(BF16)
    attended = dot(back, att[...].astype(BF16)).astype(BF16)

    @pl.when(core == 1)
    def _():
        each(0, 4, lambda i: w3_copy(i).wait_recv())

    for j in range(3):
        cols = slice(256 * j, 256 * j + 256)
        out_ref[:, cols] = dot(attended, wall[:, :, cols].reshape(WIDTH, 256)).astype(BF16)

    send_across.wait_send()
    send_sibling.wait_send()
    send_on.wait_send()
    a_all(lambda c: c.wait_send())

    @pl.when(core == 0)
    def _():
        give.wait_send()

    @pl.when(core == 1)
    def _():
        relay.wait_send()
        each(1, 4, lambda k: kv3_copy(k).wait_send())
        each(4, 16, lambda k: far_copy(k).wait_send())
        c_all(lambda c: c.wait_send())

    @pl.when(core == 0)
    def _():
        each(0, 4, lambda i: w3_copy(i).wait_send())

        for step in range(4):
            for way in range(2):
                wy_copy(step, way).wait_send()
                wf_copy(step, way).wait_send()

    def w1_left():
        w1_copy(1, 0).wait_send()
        w1_copy(3, 0).wait_send()

    bringing(0, w1_left)
    bringing(1, lambda: w1_copy(3, 1).wait_send())
    for step in range(4):
        bringing(step, lambda step=step: each(1, 4, lambda k: wx_copy(step, k).wait_send()))


def shards(tokens, tile_pos, w_qkv, w_out):
    dma = pltpu.SemaphoreType.DMA
    in_hbm = pl.BlockSpec(memory_space=pltpu.HBM)
    return pl.pallas_call(
        kernel,
        out_shape=jax.ShapeDtypeStruct((ROWS, WIDTH), BF16),
        in_specs=[in_hbm] * 4,
        out_specs=pl.BlockSpec(memory_space=pltpu.VMEM),
        scratch_shapes=[
            pltpu.VMEM((ROWS, WIDTH), BF16),
            pltpu.VMEM((2, ROWS), jnp.int32),
            pltpu.VMEM((WIDTH, 3 * WIDTH), BF16),
            pltpu.VMEM((4, ROWS, WIDTH), BF16),
            pltpu.VMEM((ROWS, WIDTH), BF16),
            pltpu.VMEM((4 * ROWS, 2 * WIDTH), BF16),
            pltpu.VMEM((HEADS, 16, 256), BF16),
            pltpu.VMEM((32, 16, 256), BF16),
            pltpu.VMEM((4, 128, 128), BF16),
            pltpu.VMEM((16, 32, 128), BF16),
            pltpu.VMEM((128, 128), BF16),
            pltpu.VMEM((512, 128), F32),
            pltpu.VMEM((32, 16, 128), BF16),
            pltpu.VMEM((HEADS, 16, 128), BF16),
            pltpu.VMEM((ROWS, WIDTH), F32),
            pltpu.VMEM((HEADS, ROWS, 128), F32),
            pltpu.VMEM((48, 16, WIDTH), BF16),
            dma((6,)), dma((3,)), dma((3,)), dma((16,)), dma, dma, dma,
            dma((4,)), dma((4,)), dma((16,)), dma((16,)), dma, dma, dma((32,)), dma,
            dma((5,)), dma((4,)), dma((4, 4)), dma((4,)), dma((4, 2)), dma((4, 2)), dma((4, 2)), dma((4, 2)), dma((4,)), dma((4,)),
            pltpu.SemaphoreType.REGULAR, pltpu.SemaphoreType.REGULAR,
        ],
        compiler_params=pltpu.CompilerParams(
            collective_id=0, has_side_effects=True, vmem_limit_bytes=60 * 1024 * 1024
        ),
        name="dilated_attention",
    )(tokens, tile_pos, w_qkv, w_out)


def solution(mesh):
    placed = (P(("grp", "seq"), None), P(None, ("grp", "seq")), P(), P("grp", None))
    return jax.shard_map(
        shards, mesh=mesh, in_specs=placed, out_specs=P(("grp", "seq"), None), check_vma=False
    )
```

```python
import jax
import jax.numpy as jnp
import numpy as np
from jax import lax
from jax.experimental import pallas as pl
from jax.experimental.pallas import tpu as pltpu
from jax.sharding import PartitionSpec as P

MESH = pl.DeviceIdType.MESH
F32 = jnp.float32
BF16 = jnp.bfloat16
ROWS = 128
WIDTH = 768
HEADS = 16
LOG2E = 1.4426950408889634
SCALE = 48 ** (-0.5) * LOG2E


def iota(shape, axis):
    return lax.broadcasted_iota(jnp.int32, shape, axis)


def dot(a, b):
    return jnp.dot(a, b, preferred_element_type=F32)


def dot_nt(a, b):
    return lax.dot_general(a, b, (((1,), (1,)), ((), ())), preferred_element_type=F32)


def row_order(p):
    return p // 16 + 8 * ((p % 4) * 4 + (p % 16) // 4)


def omega(lane):
    j = lane % 192
    rate = jnp.ones(lane.shape, F32)
    for bit in range(8):
        rate = jnp.where((j // 2**bit) % 2 == 1, rate * float(10000.0 ** (-(2**bit) / 192)), rate)
    return rate


def sine(angle, quarter_turns):
    turns = jnp.floor(angle * (2.0 / np.pi) + 0.5)
    rest = ((angle - turns * 1.5703125) - turns * 4.837512969970703125e-4) - turns * 7.54978995489188216e-8
    quadrant = turns.astype(jnp.int32) + quarter_turns
    sq = rest * rest
    sin_part = rest + rest * sq * (-1.6666654611e-1 + sq * (8.3321608736e-3 - sq * 1.9515295891e-4))
    cos_part = 1.0 - 0.5 * sq + sq * sq * (
        4.166664568298827e-2 + sq * (-1.388731625493765e-3 + sq * 2.443315711809948e-5)
    )
    value = jnp.where((quadrant & 1) == 1, cos_part, sin_part)
    return jnp.where((quadrant & 2) == 2, -value, value)


def soft(scores):
    top = jnp.max(scores, axis=1, keepdims=True)
    return top, jnp.exp2((scores - top) * SCALE)


def merge(a, l, b, m):
    gap = m - l
    share = 1.0 / (1.0 + jnp.exp2(-gap))
    both = jnp.maximum(l, m) + jnp.log2(1.0 + jnp.exp2(-jnp.abs(gap)))
    return a + (b - a) * share, both


def attend(queries, keys_values):
    top, weights = soft(dot_nt(queries, keys_values))
    mixed = dot(weights.astype(BF16), keys_values)
    total = mixed[:, 96:97]
    return mixed * (1.0 / total), top * SCALE + jnp.log2(total)


def kernel(
    tok_hbm, pos_hbm, wqkv_hbm, wout_hbm, out_ref,
    tok, pos, wq, emb, q_own, kv_all, msg, recv_a, kv3, far, q3, out2, msg_c, recv_c,
    att, lse, wall,
    load_sem, emb_send, emb_recv, a_send, a_recv,
    kv3_send, kv3_recv, far_send, far_recv, c_send, c_recv,
    w1_send, w1_recv, wx_send, wx_recv, wy_send, wy_recv, wf_send, wf_recv, w3_send, w3_recv, past,
):
    g = lax.axis_index("grp")
    s = lax.axis_index("seq")
    core = s % 2
    chip = s // 2
    x = s // 8
    zh = g // 4
    y = g % 4
    sibling = s + 1 - 2 * core
    across = s + 2 - 4 * (chip % 2)

    def remote(src, dst, send_sem, recv_sem, grp, seq):
        return pltpu.make_async_remote_copy(
            src_ref=src, dst_ref=dst, send_sem=send_sem, recv_sem=recv_sem,
            device_id=(grp, seq), device_id_type=MESH,
        )

    def each(low, high, body):
        def step(i, carry):
            body(i)
            return carry
        lax.fori_loop(low, high, step, 0)

    def seat(k):
        return ((x + 2 + k // 4) % 4) * 4 + (chip + k) % 4

    load_tok = pltpu.make_async_copy(tok_hbm, tok, load_sem.at[0])
    load_pos = pltpu.make_async_copy(pos_hbm, pos, load_sem.at[1])
    load_wq = [
        pltpu.make_async_copy(
            wqkv_hbm.at[:, pl.ds(WIDTH * i, WIDTH)], wq.at[:, pl.ds(WIDTH * i, WIDTH)], load_sem.at[2 + i]
        )
        for i in range(3)
    ]
    load_tok.start()
    load_pos.start()
    for item in load_wq:
        item.start()

    def part_at(step):
        return (x - zh - step + 8) % 4

    def block_at(step, off):
        return (((zh + step) % 4) * 4 + (y + off + 4) % 4) * 3

    load_wout = pltpu.make_async_copy(
        wout_hbm.at[pl.ds(pl.multiple_of(16 * (part_at(0) % 3), 16), 16)],
        wall.at[block_at(0, 0) + part_at(0) % 3], load_sem.at[5],
    )

    def bringing(step, act):
        pl.when((core == 0) & (part_at(step) < 3))(act)

    bringing(0, load_wout.start)

    barrier = pltpu.get_barrier_semaphore()

    def greet(grp, seq):
        pl.semaphore_signal(barrier, inc=1, device_id=(grp, seq), device_id_type=MESH)

    @pl.when(core == 1)
    def _():
        greet((g + 4) % 16, s)
        greet((g + 12) % 16, s)
        each(1, 32, lambda k: greet(g, (s + k) % 32))
        each(1, 4, lambda k: greet(zh * 4 + (y + k) % 4, s))

    @pl.when(core == 0)
    def _():
        greet((g + 4) % 16, s)
        greet((g + 12) % 16, s)
        each(0, 16, lambda k: greet(g, 2 * k + 1))
        greet(g, across)
        each(1, 4, lambda k: greet(g, ((x + k) % 4) * 8 + s % 8))
        greet(zh * 4 + (y + 1) % 4, s)
        greet(zh * 4 + (y + 3) % 4, s)

    load_tok.wait()
    load_pos.wait()
    order = (row_order(iota((ROWS, ROWS), 0)) == iota((ROWS, ROWS), 1)).astype(F32)
    place = pos[...].astype(F32)
    pos_x = jnp.sum(order * place[0:1, :], axis=1, keepdims=True)
    pos_y = jnp.sum(order * place[1:2, :], axis=1, keepdims=True)
    order_bf = order.astype(BF16)
    for i in range(6):
        cols = slice(128 * i, 128 * i + 128)
        lane = iota((1, 128), 1) + 128 * i
        spot = pos_x if i < 3 else pos_y
        turn = ((lane % 384) >= 192).astype(jnp.int32)
        value = sine(spot * omega(lane), turn)
        emb[0, :, cols] = (dot(order_bf, tok[:, cols]) + value).astype(BF16)

    for i in range(3):
        load_wq[i].wait()
        for j in range(3):
            part = dot(emb[0], wq[:, WIDTH * i + 256 * j : WIDTH * i + 256 * j + 256]).astype(BF16)
            if i == 0:
                q_own[:, 256 * j : 256 * j + 256] = part
            else:
                first = WIDTH * (i - 1) + 256 * j
                kv_all[0:ROWS, first : first + 256] = part

    lane128 = iota((1, 128), 1)
    for rho in range(8):
        base = 128 * (rho >= 3)
        off = 48 * rho - base
        src_row = iota((256, 128), 0)
        dst_lane = iota((256, 128), 1)
        put_first = ((src_row == dst_lane + off) & (dst_lane < 48)).astype(F32).astype(BF16)
        put_second = (
            (src_row == dst_lane - 48 + off) & (dst_lane >= 48) & (dst_lane < 96)
        ).astype(F32).astype(BF16)
        rows = slice(16 * rho, 16 * rho + 16)
        for e in range(2):
            h = rho + 8 * e
            w0 = 384 * e + base
            q_part = dot(q_own[rows, w0 : w0 + 256], put_first)
            kv_part = dot(kv_all[rows, w0 : w0 + 256], put_first) + dot(
                kv_all[rows, WIDTH + w0 : WIDTH + w0 + 256], put_second
            )
            kv_part = jnp.where(lane128 >= 96, 1.0, kv_part)
            msg[h, :, 0:128] = kv_part.astype(BF16)
            msg[h, :, 128:256] = q_part.astype(BF16)

    @pl.when(core == 1)
    def _():
        pl.semaphore_wait(barrier, 36)

    @pl.when(core == 0)
    def _():
        pl.semaphore_wait(barrier, 24)

    def a_copy(k):
        h = seat(k)
        return remote(msg.at[h], recv_a.at[s], a_send.at[k], a_recv, g, 2 * h + 1)

    a_local = pltpu.make_async_copy(msg.at[chip], recv_a.at[s], a_recv)

    def a_all(act):
        each(0, 8, lambda k: act(a_copy(k)))
        each(9, 16, lambda k: act(a_copy(k)))

        @pl.when(core == 0)
        def _():
            act(a_copy(8))

    a_all(lambda c: c.start())

    @pl.when(core == 1)
    def _():
        a_local.start()

    send_across = remote(emb.at[0], emb.at[2], emb_send.at[0], emb_recv.at[0], g, across)
    send_sibling = remote(emb.at[0], emb.at[1], emb_send.at[1], emb_recv.at[1], g, sibling)
    send_on = remote(emb.at[2], emb.at[3], emb_send.at[2], emb_recv.at[2], g, sibling)

    def tell(sem, grp):
        pl.semaphore_signal(sem, inc=1, device_id=(grp, s), device_id_type=MESH)

    @pl.when(core == 1)
    def _():
        tell(past, (g + 12) % 16)

    def w1_copy(k, step):
        block = wall.at[block_at(step, 0) + part_at(step) % 3]
        return remote(
            block, block, w1_send.at[k + step], w1_recv.at[(zh + step) % 4], (g + 4 * k + 16) % 16, s
        )

    def w1_wait(step):
        block = wall.at[block_at(step, 0) + part_at(step) % 3]
        pltpu.make_async_copy(block, block, w1_recv.at[(zh + step) % 4]).wait()

    def wx_copy(step, k):
        block = wall.at[block_at(step, 0) + part_at(step) % 3]
        return remote(
            block, block, wx_send.at[step, k], wx_recv.at[(zh + step) % 4], g, ((x + k) % 4) * 8 + s % 8
        )

    def wy_copy(step, way):
        blocks = wall.at[pl.ds(block_at(step, 0), 3)]
        return remote(
            blocks, blocks, wy_send.at[step, way], wy_recv.at[(zh + step) % 4, way],
            zh * 4 + (y + 1 + 2 * way) % 4, s,
        )

    def wf_copy(step, way):
        blocks = wall.at[pl.ds(block_at(step, 2 * way - 1), 3), :, pl.ds(384 * way, 384)]
        return remote(
            blocks, blocks, wf_send.at[step, way], wf_recv.at[(zh + step) % 4, way],
            zh * 4 + (y + 1 + 2 * way) % 4, s,
        )

    def w3_copy(i):
        blocks = wall.at[pl.ds(12 * i, 12)]
        return remote(blocks, blocks, w3_send.at[i], w3_recv.at[i], g, sibling)

    def wx_start(step):
        def act():
            each(1, 4, lambda k: wx_copy(step, k).start())
        bringing(step, act)

    def wy_start(step):
        sem = wx_recv.at[(zh + step) % 4]

        @pl.when(part_at(step) < 3)
        def _():
            pltpu.make_async_copy(wall.at[pl.ds(0, 2)], wall.at[pl.ds(0, 2)], sem).wait()

        @pl.when(part_at(step) == 3)
        def _():
            pltpu.make_async_copy(wall.at[pl.ds(0, 3)], wall.at[pl.ds(0, 3)], sem).wait()

        wy_copy(step, 0).start()
        wy_copy(step, 1).start()

    def wf_start(step):
        for way in range(2):
            wy_copy(step, way).wait_recv()
            wf_copy(step, way).start()

    def w3_start(step):
        for way in range(2):
            wf_copy(step, way).wait_recv()
        w3_copy((zh + step) % 4).start()

    def first_w1():
        load_wout.wait()
        w1_copy(1, 0).start()
        w1_copy(3, 0).start()

    bringing(0, first_w1)
    wx_start(0)
    send_across.start()
    send_sibling.start()

    def other_rows(slot):
        for j in range(6):
            cols = slice(256 * j, 256 * j + 256)
            kv_all[ROWS * slot : ROWS * slot + ROWS, cols] = dot(
                emb[slot], wq[:, WIDTH + 256 * j : WIDTH + 256 * j + 256]
            ).astype(BF16)

    send_sibling.wait_recv()
    other_rows(1)

    @pl.when(core == 1)
    def _():
        pl.semaphore_wait(past, 1)

    def pass_on():
        w1_wait(1)
        w1_copy(3, 1).start()

    @pl.when(core == 0)
    def _():
        wy_start(0)

    bringing(1, pass_on)
    wx_start(1)
    bringing(3, lambda: w1_wait(3))
    wx_start(3)

    e_own = chip // 8

    def kv3_copy(k):
        block = kv3.at[y]
        return remote(block, block, kv3_send.at[k], kv3_recv.at[y], zh * 4 + (y + k) % 4, s)

    def far_copy(k):
        return remote(
            kv3.at[y, pl.ds(0, 32)], far.at[4 * y + zh], far_send.at[k], far_recv.at[zh],
            ((zh + k) % 4) * 4 + y, s,
        )

    def spread_copy(k):
        slots = far.at[pl.ds(4 * y, 4)]
        return remote(slots, slots, far_send.at[k + 4], far_recv.at[4 + y], zh * 4 + (y + k) % 4, s)

    @pl.when(core == 1)
    def _():
        pltpu.make_async_copy(recv_a, recv_a, a_recv).wait()
        spot = iota((128, 512), 0)
        col = iota((128, 512), 1)
        pick = ((spot % 32) * 16 + 4 * e_own + spot // 32 == col).astype(F32).astype(BF16)
        chosen = dot(pick, recv_a[...].reshape(512, 256)).astype(BF16)
        kv3[y] = chosen[:, 0:128]
        q3[...] = chosen[:, 128:256]
        far_copy(2).start()
        far_copy(1).start()
        far_copy(3).start()
        each(1, 4, lambda k: kv3_copy(k).start())

    @pl.when(core == 0)
    def _():
        wf_start(0)
        wy_start(1)
        wy_start(3)

    send_across.wait_recv()
    send_on.start()

    @pl.when(core == 1)
    def _():
        def block(i, carry):
            rows = pl.ds(pl.multiple_of(128 * i, 128), 128)
            flat = recv_a[...].reshape(512, 256)
            queries = recv_a[pl.ds(8 * i, 8)][:, :, 128:256].reshape(128, 128)
            mixed, level = attend(queries, flat[:, 0:128])
            out2[rows, :] = jnp.where(lane128 < 48, level, mixed)
            return carry

        lax.fori_loop(0, 4, block, 0)

    bringing(2, lambda: w1_wait(2))
    wx_start(2)

    @pl.when(core == 0)
    def _():
        wf_start(1)
        wf_start(3)

    other_rows(2)
    send_on.wait_recv()
    other_rows(3)

    @pl.when(core == 0)
    def _():
        wy_start(2)
        w3_start(0)

    def first_branch(rho, carry):
        b = (rho + 5) // 8
        off = 48 * rho - 128 * b
        lane = iota((1, 256), 1)
        mine = (lane >= off) & (lane < off + 48)
        keep = mine.astype(F32).astype(BF16)
        for e in range(2):
            w0 = 384 * e + 128 * b
            win = pl.ds(pl.multiple_of(w0, 128), 256)
            win_v = pl.ds(pl.multiple_of(WIDTH + w0, 128), 256)
            top, weights = soft(dot_nt(q_own[:, win] * keep, kv_all[:, win]))
            total = jnp.sum(weights, axis=1, keepdims=True)
            mixed = dot(weights.astype(BF16), kv_all[:, win_v]) * (1.0 / total)
            att[:, win] = jnp.where(mine, mixed, att[:, win])
            lse[rho + 8 * e] = jnp.broadcast_to(top * SCALE + jnp.log2(total), (ROWS, 128))
        return carry

    @pl.when(core == 0)
    def _():
        lax.fori_loop(0, 2, first_branch, 0)
        wf_start(2)
        w3_start(1)
        w3_start(3)
        lax.fori_loop(2, 4, first_branch, 0)
        w3_start(2)

    def c_copy(k):
        there = 2 * seat(k // 2) + 1 - k % 2
        return remote(msg_c.at[there], recv_c.at[chip], c_send.at[k], c_recv, g, there)

    def c_all(act):
        each(0, 16, lambda k: act(c_copy(k)))
        each(17, 32, lambda k: act(c_copy(k)))

    @pl.when(core == 1)
    def _():
        each(1, 4, lambda k: pltpu.make_async_copy(kv3.at[0], kv3.at[0], kv3_recv.at[(y + k) % 4]).wait())
        mixed3, level3 = attend(q3[...], kv3[...].reshape(512, 128))

        def fold(m, a, l):
            rows = pl.ds(4 * e_own + m, 32, stride=16)
            held = out2[rows, :]
            a, l = merge(held, held[:, 0:1], a, l)
            out2[rows, :] = jnp.where(lane128 < 48, l, a)

        for m in range(4):
            fold(m, mixed3[32 * m : 32 * m + 32], level3[32 * m : 32 * m + 32])
        far[4 * y + zh] = kv3[y, 0:32, :]
        each(1, 4, lambda k: pltpu.make_async_copy(far.at[0], far.at[0], far_recv.at[(zh + k) % 4]).wait())
        each(1, 4, lambda k: spread_copy(k).start())
        lax.fori_loop(0, 2, first_branch, 0)
        each(1, 4, lambda k: pltpu.make_async_copy(
            far.at[pl.ds(0, 4)], far.at[pl.ds(0, 4)], far_recv.at[4 + (y + k) % 4]).wait())
        mixed4, level4 = attend(q3[0:32, :], far[...].reshape(512, 128))
        fold(0, mixed4, level4)
        done = out2[...]
        level = done[:, 0:1]
        high = level.astype(BF16).astype(F32)
        mid = (level - high).astype(BF16).astype(F32)
        low = level - high - mid
        coded = jnp.where(lane128 == 0, high, jnp.where(lane128 == 1, mid, jnp.where(lane128 == 2, low, done)))
        msg_c[...] = coded.astype(BF16).reshape(32, 16, 128)
        c_all(lambda c: c.start())
        pltpu.make_async_copy(msg_c.at[s], recv_c.at[chip], c_recv).start()

    lax.fori_loop(4 - 2 * core, 8, first_branch, 0)

    pltpu.make_async_copy(recv_c, recv_c, c_recv).wait()
    for rho in range(8):
        base = 128 * (rho >= 3)
        off = 48 * rho - base
        src_row = iota((128, 256), 0)
        dst_lane = iota((128, 256), 1)
        put_back = ((src_row - 48 + off == dst_lane) & (src_row >= 48) & (src_row < 96)).astype(F32).astype(BF16)
        add_up = (src_row < 3).astype(F32).astype(BF16)
        lane = iota((1, 256), 1)
        mine = (lane >= off) & (lane < off + 48)
        rows = slice(16 * rho, 16 * rho + 16)
        for e in range(2):
            h = rho + 8 * e
            w0 = 384 * e + base
            other = dot(recv_c[h], put_back)
            level = dot(recv_c[h], add_up)
            own_level = lse[h, rows, 0:1]
            held = att[rows, w0 : w0 + 256]
            share = 1.0 / (1.0 + jnp.exp2(own_level - level))
            att[rows, w0 : w0 + 256] = jnp.where(mine, held + (other - held) * share, held)

    back = (row_order(iota((ROWS, ROWS), 1)) == iota((ROWS, ROWS), 0)).astype(F32).astype(BF16)
    attended = dot(back, att[...].astype(BF16)).astype(BF16)

    @pl.when(core == 1)
    def _():
        each(0, 4, lambda i: w3_copy(i).wait_recv())

    for j in range(3):
        cols = slice(256 * j, 256 * j + 256)
        out_ref[:, cols] = dot(attended, wall[:, :, cols].reshape(WIDTH, 256)).astype(BF16)

    send_across.wait_send()
    send_sibling.wait_send()
    send_on.wait_send()
    a_all(lambda c: c.wait_send())

    @pl.when(core == 1)
    def _():
        each(1, 4, lambda k: kv3_copy(k).wait_send())
        each(1, 4, lambda k: far_copy(k).wait_send())
        each(1, 4, lambda k: spread_copy(k).wait_send())
        c_all(lambda c: c.wait_send())

    @pl.when(core == 0)
    def _():
        each(0, 4, lambda i: w3_copy(i).wait_send())

        for step in range(4):
            for way in range(2):
                wy_copy(step, way).wait_send()
                wf_copy(step, way).wait_send()

    def w1_left():
        w1_copy(1, 0).wait_send()
        w1_copy(3, 0).wait_send()

    bringing(0, w1_left)
    bringing(1, lambda: w1_copy(3, 1).wait_send())
    for step in range(4):
        bringing(step, lambda step=step: each(1, 4, lambda k: wx_copy(step, k).wait_send()))


def shards(tokens, tile_pos, w_qkv, w_out):
    dma = pltpu.SemaphoreType.DMA
    in_hbm = pl.BlockSpec(memory_space=pltpu.HBM)
    return pl.pallas_call(
        kernel,
        out_shape=jax.ShapeDtypeStruct((ROWS, WIDTH), BF16),
        in_specs=[in_hbm] * 4,
        out_specs=pl.BlockSpec(memory_space=pltpu.VMEM),
        scratch_shapes=[
            pltpu.VMEM((ROWS, WIDTH), BF16),
            pltpu.VMEM((2, ROWS), jnp.int32),
            pltpu.VMEM((WIDTH, 3 * WIDTH), BF16),
            pltpu.VMEM((4, ROWS, WIDTH), BF16),
            pltpu.VMEM((ROWS, WIDTH), BF16),
            pltpu.VMEM((4 * ROWS, 2 * WIDTH), BF16),
            pltpu.VMEM((HEADS, 16, 256), BF16),
            pltpu.VMEM((32, 16, 256), BF16),
            pltpu.VMEM((4, 128, 128), BF16),
            pltpu.VMEM((16, 32, 128), BF16),
            pltpu.VMEM((128, 128), BF16),
            pltpu.VMEM((512, 128), F32),
            pltpu.VMEM((32, 16, 128), BF16),
            pltpu.VMEM((HEADS, 16, 128), BF16),
            pltpu.VMEM((ROWS, WIDTH), F32),
            pltpu.VMEM((HEADS, ROWS, 128), F32),
            pltpu.VMEM((48, 16, WIDTH), BF16),
            dma((6,)), dma((3,)), dma((3,)), dma((16,)), dma,
            dma((4,)), dma((4,)), dma((8,)), dma((8,)), dma((32,)), dma,
            dma((5,)), dma((4,)), dma((4, 4)), dma((4,)), dma((4, 2)), dma((4, 2)), dma((4, 2)), dma((4, 2)), dma((4,)), dma((4,)),
            pltpu.SemaphoreType.REGULAR,
        ],
        compiler_params=pltpu.CompilerParams(
            collective_id=0, has_side_effects=True, vmem_limit_bytes=60 * 1024 * 1024
        ),
        name="dilated_attention",
    )(tokens, tile_pos, w_qkv, w_out)


def solution(mesh):
    placed = (P(("grp", "seq"), None), P(None, ("grp", "seq")), P(), P("grp", None))
    return jax.shard_map(
        shards, mesh=mesh, in_specs=placed, out_specs=P(("grp", "seq"), None), check_vma=False
    )
```

```python
import jax
import jax.numpy as jnp
import numpy as np
from jax import lax
from jax.experimental import pallas as pl
from jax.experimental.pallas import tpu as pltpu
from jax.sharding import PartitionSpec as P

MESH = pl.DeviceIdType.MESH
F32 = jnp.float32
BF16 = jnp.bfloat16
ROWS = 128
WIDTH = 768
HEADS = 16
LOG2E = 1.4426950408889634
SCALE = 48 ** (-0.5) * LOG2E


def iota(shape, axis):
    return lax.broadcasted_iota(jnp.int32, shape, axis)


def dot(a, b):
    return jnp.dot(a, b, preferred_element_type=F32)


def dot_nt(a, b):
    return lax.dot_general(a, b, (((1,), (1,)), ((), ())), preferred_element_type=F32)


def row_order(p):
    return p // 16 + 8 * ((p % 4) * 4 + (p % 16) // 4)


def omega(lane):
    j = lane % 192
    rate = jnp.ones(lane.shape, F32)
    for bit in range(8):
        rate = jnp.where((j // 2**bit) % 2 == 1, rate * float(10000.0 ** (-(2**bit) / 192)), rate)
    return rate


def sine(angle, quarter_turns):
    turns = jnp.floor(angle * (2.0 / np.pi) + 0.5)
    rest = ((angle - turns * 1.5703125) - turns * 4.837512969970703125e-4) - turns * 7.54978995489188216e-8
    quadrant = turns.astype(jnp.int32) + quarter_turns
    sq = rest * rest
    sin_part = rest + rest * sq * (-1.6666654611e-1 + sq * (8.3321608736e-3 - sq * 1.9515295891e-4))
    cos_part = 1.0 - 0.5 * sq + sq * sq * (
        4.166664568298827e-2 + sq * (-1.388731625493765e-3 + sq * 2.443315711809948e-5)
    )
    value = jnp.where((quadrant & 1) == 1, cos_part, sin_part)
    return jnp.where((quadrant & 2) == 2, -value, value)


def soft(scores):
    top = jnp.max(scores, axis=1, keepdims=True)
    return top, jnp.exp2((scores - top) * SCALE)


def merge(a, l, b, m):
    gap = m - l
    share = 1.0 / (1.0 + jnp.exp2(-gap))
    both = jnp.maximum(l, m) + jnp.log2(1.0 + jnp.exp2(-jnp.abs(gap)))
    return a + (b - a) * share, both


def attend(queries, keys_values):
    top, weights = soft(dot_nt(queries, keys_values))
    mixed = dot(weights.astype(BF16), keys_values)
    total = mixed[:, 96:97]
    return mixed * (1.0 / total), top * SCALE + jnp.log2(total)


def kernel(
    tok_hbm, pos_hbm, wqkv_hbm, wout_hbm, out_ref,
    tok, pos, wq, emb, q_own, kv_all, msg, recv_a, kv3, far, q3, out2, msg_c, recv_c,
    att, lse, wall,
    load_sem, emb_send, emb_recv, a_send, a_recv,
    kv3_send, kv3_recv, far_send, far_recv, c_send, c_recv,
    w1_send, w1_recv, wx_send, wx_recv, wy_send, wy_recv, wf_send, wf_recv, w3_send, w3_recv, past,
):
    g = lax.axis_index("grp")
    s = lax.axis_index("seq")
    core = s % 2
    chip = s // 2
    x = s // 8
    zh = g // 4
    y = g % 4
    sibling = s + 1 - 2 * core
    across = s + 2 - 4 * (chip % 2)

    def remote(src, dst, send_sem, recv_sem, grp, seq):
        return pltpu.make_async_remote_copy(
            src_ref=src, dst_ref=dst, send_sem=send_sem, recv_sem=recv_sem,
            device_id=(grp, seq), device_id_type=MESH,
        )

    def each(low, high, body):
        def step(i, carry):
            body(i)
            return carry
        lax.fori_loop(low, high, step, 0)

    def seat(k):
        return ((x + 2 + k // 4) % 4) * 4 + (chip + k) % 4

    load_tok = pltpu.make_async_copy(tok_hbm, tok, load_sem.at[0])
    load_pos = pltpu.make_async_copy(pos_hbm, pos, load_sem.at[1])
    load_wq = [
        pltpu.make_async_copy(
            wqkv_hbm.at[:, pl.ds(WIDTH * i, WIDTH)], wq.at[:, pl.ds(WIDTH * i, WIDTH)], load_sem.at[2 + i]
        )
        for i in range(3)
    ]
    load_tok.start()
    load_pos.start()
    for item in load_wq:
        item.start()

    def part_at(step):
        return (x - zh - step + 8) % 4

    def block_at(step, off):
        return (((zh + step) % 4) * 4 + (y + off + 4) % 4) * 3

    load_wout = pltpu.make_async_copy(
        wout_hbm.at[pl.ds(pl.multiple_of(16 * (part_at(0) % 3), 16), 16)],
        wall.at[block_at(0, 0) + part_at(0) % 3], load_sem.at[5],
    )

    def bringing(step, act):
        pl.when((core == 0) & (part_at(step) < 3))(act)

    bringing(0, load_wout.start)

    barrier = pltpu.get_barrier_semaphore()

    def greet(grp, seq):
        pl.semaphore_signal(barrier, inc=1, device_id=(grp, seq), device_id_type=MESH)

    @pl.when(core == 1)
    def _():
        greet((g + 4) % 16, s)
        greet((g + 12) % 16, s)
        each(1, 32, lambda k: greet(g, (s + k) % 32))
        each(1, 4, lambda k: greet(zh * 4 + (y + k) % 4, s))

    @pl.when(core == 0)
    def _():
        greet((g + 4) % 16, s)
        greet((g + 12) % 16, s)
        each(0, 16, lambda k: greet(g, 2 * k + 1))
        greet(g, across)
        each(1, 4, lambda k: greet(g, ((x + k) % 4) * 8 + s % 8))
        greet(zh * 4 + (y + 1) % 4, s)
        greet(zh * 4 + (y + 3) % 4, s)

    load_tok.wait()
    load_pos.wait()
    order = (row_order(iota((ROWS, ROWS), 0)) == iota((ROWS, ROWS), 1)).astype(F32)
    place = pos[...].astype(F32)
    pos_x = jnp.sum(order * place[0:1, :], axis=1, keepdims=True)
    pos_y = jnp.sum(order * place[1:2, :], axis=1, keepdims=True)
    order_bf = order.astype(BF16)
    for i in range(6):
        cols = slice(128 * i, 128 * i + 128)
        lane = iota((1, 128), 1) + 128 * i
        spot = pos_x if i < 3 else pos_y
        turn = ((lane % 384) >= 192).astype(jnp.int32)
        value = sine(spot * omega(lane), turn)
        emb[0, :, cols] = (dot(order_bf, tok[:, cols]) + value).astype(BF16)

    def w1_copy(k, step):
        block = wall.at[block_at(step, 0) + part_at(step) % 3]
        return remote(
            block, block, w1_send.at[k + step], w1_recv.at[(zh + step) % 4], (g + 4 * k + 16) % 16, s
        )

    def w1_wait(step):
        block = wall.at[block_at(step, 0) + part_at(step) % 3]
        pltpu.make_async_copy(block, block, w1_recv.at[(zh + step) % 4]).wait()

    def wx_copy(step, k):
        block = wall.at[block_at(step, 0) + part_at(step) % 3]
        return remote(
            block, block, wx_send.at[step, k], wx_recv.at[(zh + step) % 4], g, ((x + k) % 4) * 8 + s % 8
        )

    def wy_copy(step, way):
        blocks = wall.at[pl.ds(block_at(step, 0), 3)]
        return remote(
            blocks, blocks, wy_send.at[step, way], wy_recv.at[(zh + step) % 4, way],
            zh * 4 + (y + 1 + 2 * way) % 4, s,
        )

    def wf_copy(step, way):
        blocks = wall.at[pl.ds(block_at(step, 2 * way - 1), 3), :, pl.ds(384 * way, 384)]
        return remote(
            blocks, blocks, wf_send.at[step, way], wf_recv.at[(zh + step) % 4, way],
            zh * 4 + (y + 1 + 2 * way) % 4, s,
        )

    def w3_copy(i):
        blocks = wall.at[pl.ds(12 * i, 12)]
        return remote(blocks, blocks, w3_send.at[i], w3_recv.at[i], g, sibling)

    def wx_start(step):
        def act():
            each(1, 4, lambda k: wx_copy(step, k).start())
        bringing(step, act)

    def wy_start(step):
        sem = wx_recv.at[(zh + step) % 4]

        @pl.when(part_at(step) < 3)
        def _():
            pltpu.make_async_copy(wall.at[pl.ds(0, 2)], wall.at[pl.ds(0, 2)], sem).wait()

        @pl.when(part_at(step) == 3)
        def _():
            pltpu.make_async_copy(wall.at[pl.ds(0, 3)], wall.at[pl.ds(0, 3)], sem).wait()

        wy_copy(step, 0).start()
        wy_copy(step, 1).start()

    def wf_start(step):
        for way in range(2):
            wy_copy(step, way).wait_recv()
            wf_copy(step, way).start()

    def w3_start(step):
        for way in range(2):
            wf_copy(step, way).wait_recv()
        w3_copy((zh + step) % 4).start()

    def first_w1():
        load_wout.wait()
        w1_copy(1, 0).start()
        w1_copy(3, 0).start()

    @pl.when(core == 0)
    def _():
        pl.semaphore_wait(barrier, 24)

    bringing(0, first_w1)
    wx_start(0)

    for i in range(3):
        load_wq[i].wait()
        for j in range(3):
            part = dot(emb[0], wq[:, WIDTH * i + 256 * j : WIDTH * i + 256 * j + 256]).astype(BF16)
            if i == 0:
                q_own[:, 256 * j : 256 * j + 256] = part
            else:
                first = WIDTH * (i - 1) + 256 * j
                kv_all[0:ROWS, first : first + 256] = part

    lane128 = iota((1, 128), 1)
    for rho in range(8):
        base = 128 * (rho >= 3)
        off = 48 * rho - base
        src_row = iota((256, 128), 0)
        dst_lane = iota((256, 128), 1)
        put_first = ((src_row == dst_lane + off) & (dst_lane < 48)).astype(F32).astype(BF16)
        put_second = (
            (src_row == dst_lane - 48 + off) & (dst_lane >= 48) & (dst_lane < 96)
        ).astype(F32).astype(BF16)
        rows = slice(16 * rho, 16 * rho + 16)
        for e in range(2):
            h = rho + 8 * e
            w0 = 384 * e + base
            q_part = dot(q_own[rows, w0 : w0 + 256], put_first)
            kv_part = dot(kv_all[rows, w0 : w0 + 256], put_first) + dot(
                kv_all[rows, WIDTH + w0 : WIDTH + w0 + 256], put_second
            )
            kv_part = jnp.where(lane128 >= 96, 1.0, kv_part)
            msg[h, :, 0:128] = kv_part.astype(BF16)
            msg[h, :, 128:256] = q_part.astype(BF16)

    @pl.when(core == 1)
    def _():
        pl.semaphore_wait(barrier, 36)

    def a_copy(k):
        h = seat(k)
        return remote(msg.at[h], recv_a.at[s], a_send.at[k], a_recv, g, 2 * h + 1)

    a_local = pltpu.make_async_copy(msg.at[chip], recv_a.at[s], a_recv)

    def a_all(act):
        each(0, 8, lambda k: act(a_copy(k)))
        each(9, 16, lambda k: act(a_copy(k)))

        @pl.when(core == 0)
        def _():
            act(a_copy(8))

    a_all(lambda c: c.start())

    @pl.when(core == 1)
    def _():
        a_local.start()

    send_across = remote(emb.at[0], emb.at[2], emb_send.at[0], emb_recv.at[0], g, across)
    send_sibling = remote(emb.at[0], emb.at[1], emb_send.at[1], emb_recv.at[1], g, sibling)
    send_on = remote(emb.at[2], emb.at[3], emb_send.at[2], emb_recv.at[2], g, sibling)

    def tell(sem, grp):
        pl.semaphore_signal(sem, inc=1, device_id=(grp, s), device_id_type=MESH)

    @pl.when(core == 1)
    def _():
        tell(past, (g + 12) % 16)

    send_across.start()
    send_sibling.start()

    def other_rows(slot):
        for j in range(6):
            cols = slice(256 * j, 256 * j + 256)
            kv_all[ROWS * slot : ROWS * slot + ROWS, cols] = dot(
                emb[slot], wq[:, WIDTH + 256 * j : WIDTH + 256 * j + 256]
            ).astype(BF16)

    send_sibling.wait_recv()
    other_rows(1)

    @pl.when(core == 1)
    def _():
        pl.semaphore_wait(past, 1)

    def pass_on():
        w1_wait(1)
        w1_copy(3, 1).start()

    @pl.when(core == 0)
    def _():
        wy_start(0)

    bringing(1, pass_on)
    wx_start(1)
    bringing(3, lambda: w1_wait(3))
    wx_start(3)

    e_own = chip // 8

    def kv3_copy(k):
        block = kv3.at[y]
        return remote(block, block, kv3_send.at[k], kv3_recv.at[y], zh * 4 + (y + k) % 4, s)

    def far_copy(k):
        return remote(
            kv3.at[y, pl.ds(0, 32)], far.at[4 * y + zh], far_send.at[k], far_recv.at[zh],
            ((zh + k) % 4) * 4 + y, s,
        )

    def spread_copy(k):
        slots = far.at[pl.ds(4 * y, 4)]
        return remote(slots, slots, far_send.at[k + 4], far_recv.at[4 + y], zh * 4 + (y + k) % 4, s)

    @pl.when(core == 1)
    def _():
        pltpu.make_async_copy(recv_a, recv_a, a_recv).wait()
        spot = iota((128, 512), 0)
        col = iota((128, 512), 1)
        pick = ((spot % 32) * 16 + 4 * e_own + spot // 32 == col).astype(F32).astype(BF16)
        chosen = dot(pick, recv_a[...].reshape(512, 256)).astype(BF16)
        kv3[y] = chosen[:, 0:128]
        q3[...] = chosen[:, 128:256]
        far_copy(2).start()
        far_copy(1).start()
        far_copy(3).start()
        each(1, 4, lambda k: kv3_copy(k).start())

    @pl.when(core == 0)
    def _():
        wf_start(0)
        wy_start(1)
        wy_start(3)

    send_across.wait_recv()
    send_on.start()

    @pl.when(core == 1)
    def _():
        def block(i, carry):
            rows = pl.ds(pl.multiple_of(128 * i, 128), 128)
            flat = recv_a[...].reshape(512, 256)
            queries = recv_a[pl.ds(8 * i, 8)][:, :, 128:256].reshape(128, 128)
            mixed, level = attend(queries, flat[:, 0:128])
            out2[rows, :] = jnp.where(lane128 < 48, level, mixed)
            return carry

        lax.fori_loop(0, 4, block, 0)

    bringing(2, lambda: w1_wait(2))
    wx_start(2)

    @pl.when(core == 0)
    def _():
        wf_start(1)
        wf_start(3)

    other_rows(2)
    send_on.wait_recv()
    other_rows(3)

    @pl.when(core == 0)
    def _():
        wy_start(2)
        w3_start(0)

    def first_branch(pair, carry):
        heads_of(2 * pair)
        heads_of(2 * pair + 1)
        return carry

    def heads_of(rho):
        b = (rho + 5) // 8
        off = 48 * rho - 128 * b
        lane = iota((1, 256), 1)
        mine = (lane >= off) & (lane < off + 48)
        keep = mine.astype(F32).astype(BF16)
        for e in range(2):
            w0 = 384 * e + 128 * b
            win = pl.ds(pl.multiple_of(w0, 128), 256)
            win_v = pl.ds(pl.multiple_of(WIDTH + w0, 128), 256)
            top, weights = soft(dot_nt(q_own[:, win] * keep, kv_all[:, win]))
            total = jnp.sum(weights, axis=1, keepdims=True)
            mixed = dot(weights.astype(BF16), kv_all[:, win_v]) * (1.0 / total)
            att[:, win] = jnp.where(mine, mixed, att[:, win])
            lse[rho + 8 * e] = jnp.broadcast_to(top * SCALE + jnp.log2(total), (ROWS, 128))

    @pl.when(core == 0)
    def _():
        lax.fori_loop(0, 1, first_branch, 0)
        wf_start(2)
        w3_start(1)
        w3_start(3)
        lax.fori_loop(1, 2, first_branch, 0)
        w3_start(2)

    def c_copy(k):
        there = 2 * seat(k // 2) + 1 - k % 2
        return remote(msg_c.at[there], recv_c.at[chip], c_send.at[k], c_recv, g, there)

    def c_all(act):
        each(0, 16, lambda k: act(c_copy(k)))
        each(17, 32, lambda k: act(c_copy(k)))

    @pl.when(core == 1)
    def _():
        each(1, 4, lambda k: pltpu.make_async_copy(kv3.at[0], kv3.at[0], kv3_recv.at[(y + k) % 4]).wait())
        mixed3, level3 = attend(q3[...], kv3[...].reshape(512, 128))

        def fold(m, a, l):
            rows = pl.ds(4 * e_own + m, 32, stride=16)
            held = out2[rows, :]
            a, l = merge(held, held[:, 0:1], a, l)
            out2[rows, :] = jnp.where(lane128 < 48, l, a)

        for m in range(4):
            fold(m, mixed3[32 * m : 32 * m + 32], level3[32 * m : 32 * m + 32])
        far[4 * y + zh] = kv3[y, 0:32, :]
        lax.fori_loop(0, 1, first_branch, 0)
        each(1, 4, lambda k: pltpu.make_async_copy(far.at[0], far.at[0], far_recv.at[(zh + k) % 4]).wait())
        each(1, 4, lambda k: spread_copy(k).start())
        lax.fori_loop(1, 2, first_branch, 0)
        each(1, 4, lambda k: pltpu.make_async_copy(
            far.at[pl.ds(0, 4)], far.at[pl.ds(0, 4)], far_recv.at[4 + (y + k) % 4]).wait())
        mixed4, level4 = attend(q3[0:32, :], far[...].reshape(512, 128))
        fold(0, mixed4, level4)
        done = out2[...]
        level = done[:, 0:1]
        high = level.astype(BF16).astype(F32)
        mid = (level - high).astype(BF16).astype(F32)
        low = level - high - mid
        coded = jnp.where(lane128 == 0, high, jnp.where(lane128 == 1, mid, jnp.where(lane128 == 2, low, done)))
        msg_c[...] = coded.astype(BF16).reshape(32, 16, 128)
        c_all(lambda c: c.start())
        pltpu.make_async_copy(msg_c.at[s], recv_c.at[chip], c_recv).start()

    lax.fori_loop(2, 4, first_branch, 0)

    pltpu.make_async_copy(recv_c, recv_c, c_recv).wait()
    for rho in range(8):
        base = 128 * (rho >= 3)
        off = 48 * rho - base
        src_row = iota((128, 256), 0)
        dst_lane = iota((128, 256), 1)
        put_back = ((src_row - 48 + off == dst_lane) & (src_row >= 48) & (src_row < 96)).astype(F32).astype(BF16)
        add_up = (src_row < 3).astype(F32).astype(BF16)
        lane = iota((1, 256), 1)
        mine = (lane >= off) & (lane < off + 48)
        rows = slice(16 * rho, 16 * rho + 16)
        for e in range(2):
            h = rho + 8 * e
            w0 = 384 * e + base
            other = dot(recv_c[h], put_back)
            level = dot(recv_c[h], add_up)
            own_level = lse[h, rows, 0:1]
            held = att[rows, w0 : w0 + 256]
            share = 1.0 / (1.0 + jnp.exp2(own_level - level))
            att[rows, w0 : w0 + 256] = jnp.where(mine, held + (other - held) * share, held)

    back = (row_order(iota((ROWS, ROWS), 1)) == iota((ROWS, ROWS), 0)).astype(F32).astype(BF16)
    attended = dot(back, att[...].astype(BF16)).astype(BF16)

    @pl.when(core == 1)
    def _():
        each(0, 4, lambda i: w3_copy(i).wait_recv())

    for j in range(3):
        cols = slice(256 * j, 256 * j + 256)
        out_ref[:, cols] = dot(attended, wall[:, :, cols].reshape(WIDTH, 256)).astype(BF16)

    send_across.wait_send()
    send_sibling.wait_send()
    send_on.wait_send()
    a_all(lambda c: c.wait_send())

    @pl.when(core == 1)
    def _():
        each(1, 4, lambda k: kv3_copy(k).wait_send())
        each(1, 4, lambda k: far_copy(k).wait_send())
        each(1, 4, lambda k: spread_copy(k).wait_send())
        c_all(lambda c: c.wait_send())

    @pl.when(core == 0)
    def _():
        each(0, 4, lambda i: w3_copy(i).wait_send())

        for step in range(4):
            for way in range(2):
                wy_copy(step, way).wait_send()
                wf_copy(step, way).wait_send()

    def w1_left():
        w1_copy(1, 0).wait_send()
        w1_copy(3, 0).wait_send()

    bringing(0, w1_left)
    bringing(1, lambda: w1_copy(3, 1).wait_send())
    for step in range(4):
        bringing(step, lambda step=step: each(1, 4, lambda k: wx_copy(step, k).wait_send()))


def shards(tokens, tile_pos, w_qkv, w_out):
    dma = pltpu.SemaphoreType.DMA
    in_hbm = pl.BlockSpec(memory_space=pltpu.HBM)
    return pl.pallas_call(
        kernel,
        out_shape=jax.ShapeDtypeStruct((ROWS, WIDTH), BF16),
        in_specs=[in_hbm] * 4,
        out_specs=pl.BlockSpec(memory_space=pltpu.VMEM),
        scratch_shapes=[
            pltpu.VMEM((ROWS, WIDTH), BF16),
            pltpu.VMEM((2, ROWS), jnp.int32),
            pltpu.VMEM((WIDTH, 3 * WIDTH), BF16),
            pltpu.VMEM((4, ROWS, WIDTH), BF16),
            pltpu.VMEM((ROWS, WIDTH), BF16),
            pltpu.VMEM((4 * ROWS, 2 * WIDTH), BF16),
            pltpu.VMEM((HEADS, 16, 256), BF16),
            pltpu.VMEM((32, 16, 256), BF16),
            pltpu.VMEM((4, 128, 128), BF16),
            pltpu.VMEM((16, 32, 128), BF16),
            pltpu.VMEM((128, 128), BF16),
            pltpu.VMEM((512, 128), F32),
            pltpu.VMEM((32, 16, 128), BF16),
            pltpu.VMEM((HEADS, 16, 128), BF16),
            pltpu.VMEM((ROWS, WIDTH), F32),
            pltpu.VMEM((HEADS, ROWS, 128), F32),
            pltpu.VMEM((48, 16, WIDTH), BF16),
            dma((6,)), dma((3,)), dma((3,)), dma((16,)), dma,
            dma((4,)), dma((4,)), dma((8,)), dma((8,)), dma((32,)), dma,
            dma((5,)), dma((4,)), dma((4, 4)), dma((4,)), dma((4, 2)), dma((4, 2)), dma((4, 2)), dma((4, 2)), dma((4,)), dma((4,)),
            pltpu.SemaphoreType.REGULAR,
        ],
        compiler_params=pltpu.CompilerParams(
            collective_id=0, has_side_effects=True, vmem_limit_bytes=60 * 1024 * 1024
        ),
        name="dilated_attention",
    )(tokens, tile_pos, w_qkv, w_out)


def solution(mesh):
    placed = (P(("grp", "seq"), None), P(None, ("grp", "seq")), P(), P("grp", None))
    return jax.shard_map(
        shards, mesh=mesh, in_specs=placed, out_specs=P(("grp", "seq"), None), check_vma=False
    )
```

```python
import jax
import jax.numpy as jnp
import numpy as np
from jax import lax
from jax.experimental import pallas as pl
from jax.experimental.pallas import tpu as pltpu
from jax.sharding import PartitionSpec as P

MESH = pl.DeviceIdType.MESH
F32 = jnp.float32
BF16 = jnp.bfloat16
ROWS = 128
WIDTH = 768
HEADS = 16
LOG2E = 1.4426950408889634
SCALE = 48 ** (-0.5) * LOG2E


def iota(shape, axis):
    return lax.broadcasted_iota(jnp.int32, shape, axis)


def dot(a, b):
    return jnp.dot(a, b, preferred_element_type=F32)


def dot_nt(a, b):
    return lax.dot_general(a, b, (((1,), (1,)), ((), ())), preferred_element_type=F32)


def row_order(p):
    return p // 16 + 8 * ((p % 4) * 4 + (p % 16) // 4)


def omega(lane):
    j = lane % 192
    rate = jnp.ones(lane.shape, F32)
    for bit in range(8):
        rate = jnp.where((j // 2**bit) % 2 == 1, rate * float(10000.0 ** (-(2**bit) / 192)), rate)
    return rate


def sine(angle, quarter_turns):
    turns = jnp.floor(angle * (2.0 / np.pi) + 0.5)
    rest = ((angle - turns * 1.5703125) - turns * 4.837512969970703125e-4) - turns * 7.54978995489188216e-8
    quadrant = turns.astype(jnp.int32) + quarter_turns
    sq = rest * rest
    sin_part = rest + rest * sq * (-1.6666654611e-1 + sq * (8.3321608736e-3 - sq * 1.9515295891e-4))
    cos_part = 1.0 - 0.5 * sq + sq * sq * (
        4.166664568298827e-2 + sq * (-1.388731625493765e-3 + sq * 2.443315711809948e-5)
    )
    value = jnp.where((quadrant & 1) == 1, cos_part, sin_part)
    return jnp.where((quadrant & 2) == 2, -value, value)


def soft(scores):
    top = jnp.max(scores, axis=1, keepdims=True)
    return top, jnp.exp2((scores - top) * SCALE)


def merge(a, l, b, m):
    gap = m - l
    share = 1.0 / (1.0 + jnp.exp2(-gap))
    both = jnp.maximum(l, m) + jnp.log2(1.0 + jnp.exp2(-jnp.abs(gap)))
    return a + (b - a) * share, both


def attend(queries, keys_values):
    top, weights = soft(dot_nt(queries, keys_values))
    mixed = dot(weights.astype(BF16), keys_values)
    total = mixed[:, 96:97]
    return mixed * (1.0 / total), top * SCALE + jnp.log2(total)


def kernel(
    tok_hbm, pos_hbm, wqkv_hbm, wout_hbm, out_ref,
    tok, pos, wq, emb, q_own, kv_all, msg, recv_a, kv3, far, q3, out2, msg_c, recv_c,
    att, lse, wall,
    load_sem, emb_send, emb_recv, a_send, a_recv,
    kv3_send, kv3_recv, far_send, far_recv, c_send, c_recv,
    w1_send, w1_recv, wx_send, wx_recv, wy_send, wy_recv, wf_send, wf_recv, w3_send, w3_recv, past,
):
    g = lax.axis_index("grp")
    s = lax.axis_index("seq")
    core = s % 2
    chip = s // 2
    x = s // 8
    zh = g // 4
    y = g % 4
    sibling = s + 1 - 2 * core
    across = s + 2 - 4 * (chip % 2)

    def remote(src, dst, send_sem, recv_sem, grp, seq):
        return pltpu.make_async_remote_copy(
            src_ref=src, dst_ref=dst, send_sem=send_sem, recv_sem=recv_sem,
            device_id=(grp, seq), device_id_type=MESH,
        )

    def each(low, high, body):
        def step(i, carry):
            body(i)
            return carry
        lax.fori_loop(low, high, step, 0)

    def seat(k):
        return ((x + 2 + k // 4) % 4) * 4 + (chip + k) % 4

    load_tok = pltpu.make_async_copy(tok_hbm, tok, load_sem.at[0])
    load_pos = pltpu.make_async_copy(pos_hbm, pos, load_sem.at[1])
    load_wq = [
        pltpu.make_async_copy(
            wqkv_hbm.at[:, pl.ds(WIDTH * i, WIDTH)], wq.at[:, pl.ds(WIDTH * i, WIDTH)], load_sem.at[2 + i]
        )
        for i in range(3)
    ]
    load_tok.start()
    load_pos.start()
    for item in load_wq:
        item.start()

    def part_at(step):
        return (x - zh - step + 8) % 4

    def block_at(step, off):
        return (((zh + step) % 4) * 4 + (y + off + 4) % 4) * 3

    load_wout = pltpu.make_async_copy(
        wout_hbm.at[pl.ds(pl.multiple_of(16 * (part_at(0) % 3), 16), 16)],
        wall.at[block_at(0, 0) + part_at(0) % 3], load_sem.at[5],
    )

    def bringing(step, act):
        pl.when((core == 0) & (part_at(step) < 3))(act)

    bringing(0, load_wout.start)

    barrier = pltpu.get_barrier_semaphore()

    def greet(grp, seq):
        pl.semaphore_signal(barrier, inc=1, device_id=(grp, seq), device_id_type=MESH)

    @pl.when(core == 1)
    def _():
        greet((g + 4) % 16, s)
        greet((g + 12) % 16, s)
        each(1, 32, lambda k: greet(g, (s + k) % 32))
        each(1, 4, lambda k: greet(zh * 4 + (y + k) % 4, s))

    @pl.when(core == 0)
    def _():
        greet((g + 4) % 16, s)
        greet((g + 12) % 16, s)
        each(0, 16, lambda k: greet(g, 2 * k + 1))
        greet(g, across)
        each(1, 4, lambda k: greet(g, ((x + k) % 4) * 8 + s % 8))
        greet(zh * 4 + (y + 1) % 4, s)
        greet(zh * 4 + (y + 3) % 4, s)

    load_tok.wait()
    load_pos.wait()
    order = (row_order(iota((ROWS, ROWS), 0)) == iota((ROWS, ROWS), 1)).astype(F32)
    place = pos[...].astype(F32)
    pos_x = jnp.sum(order * place[0:1, :], axis=1, keepdims=True)
    pos_y = jnp.sum(order * place[1:2, :], axis=1, keepdims=True)
    order_bf = order.astype(BF16)
    for i in range(6):
        cols = slice(128 * i, 128 * i + 128)
        lane = iota((1, 128), 1) + 128 * i
        spot = pos_x if i < 3 else pos_y
        turn = ((lane % 384) >= 192).astype(jnp.int32)
        value = sine(spot * omega(lane), turn)
        emb[0, :, cols] = (dot(order_bf, tok[:, cols]) + value).astype(BF16)

    def w1_copy(k, step):
        block = wall.at[block_at(step, 0) + part_at(step) % 3]
        return remote(
            block, block, w1_send.at[k + step], w1_recv.at[(zh + step) % 4], (g + 4 * k + 16) % 16, s
        )

    def w1_wait(step):
        block = wall.at[block_at(step, 0) + part_at(step) % 3]
        pltpu.make_async_copy(block, block, w1_recv.at[(zh + step) % 4]).wait()

    def wx_copy(step, k):
        block = wall.at[block_at(step, 0) + part_at(step) % 3]
        return remote(
            block, block, wx_send.at[step, k], wx_recv.at[(zh + step) % 4], g, ((x + k) % 4) * 8 + s % 8
        )

    def wy_copy(step, way):
        blocks = wall.at[pl.ds(block_at(step, 0), 3)]
        return remote(
            blocks, blocks, wy_send.at[step, way], wy_recv.at[(zh + step) % 4, way],
            zh * 4 + (y + 1 + 2 * way) % 4, s,
        )

    def wf_copy(step, way):
        blocks = wall.at[pl.ds(block_at(step, 2 * way - 1), 3), :, pl.ds(384 * way, 384)]
        return remote(
            blocks, blocks, wf_send.at[step, way], wf_recv.at[(zh + step) % 4, way],
            zh * 4 + (y + 1 + 2 * way) % 4, s,
        )

    def w3_copy(i):
        blocks = wall.at[pl.ds(12 * i, 12)]
        return remote(blocks, blocks, w3_send.at[i], w3_recv.at[i], g, sibling)

    def wx_start(step):
        def act():
            each(1, 4, lambda k: wx_copy(step, k).start())
        bringing(step, act)

    def wy_start(step):
        sem = wx_recv.at[(zh + step) % 4]

        @pl.when(part_at(step) < 3)
        def _():
            pltpu.make_async_copy(wall.at[pl.ds(0, 2)], wall.at[pl.ds(0, 2)], sem).wait()

        @pl.when(part_at(step) == 3)
        def _():
            pltpu.make_async_copy(wall.at[pl.ds(0, 3)], wall.at[pl.ds(0, 3)], sem).wait()

        wy_copy(step, 0).start()
        wy_copy(step, 1).start()

    def wf_start(step):
        for way in range(2):
            wy_copy(step, way).wait_recv()
            wf_copy(step, way).start()

    def w3_start(step):
        for way in range(2):
            wf_copy(step, way).wait_recv()
        w3_copy((zh + step) % 4).start()

    def first_w1():
        load_wout.wait()
        w1_copy(1, 0).start()
        w1_copy(3, 0).start()

    @pl.when(core == 0)
    def _():
        pl.semaphore_wait(barrier, 24)

    bringing(0, first_w1)
    wx_start(0)

    for i in range(3):
        load_wq[i].wait()
        for j in range(3):
            part = dot(emb[0], wq[:, WIDTH * i + 256 * j : WIDTH * i + 256 * j + 256]).astype(BF16)
            if i == 0:
                q_own[:, 256 * j : 256 * j + 256] = part
            else:
                first = WIDTH * (i - 1) + 256 * j
                kv_all[0:ROWS, first : first + 256] = part

    lane128 = iota((1, 128), 1)
    for rho in range(8):
        base = 128 * (rho >= 3)
        off = 48 * rho - base
        src_row = iota((256, 128), 0)
        dst_lane = iota((256, 128), 1)
        put_first = ((src_row == dst_lane + off) & (dst_lane < 48)).astype(F32).astype(BF16)
        put_second = (
            (src_row == dst_lane - 48 + off) & (dst_lane >= 48) & (dst_lane < 96)
        ).astype(F32).astype(BF16)
        rows = slice(16 * rho, 16 * rho + 16)
        for e in range(2):
            h = rho + 8 * e
            w0 = 384 * e + base
            q_part = dot(q_own[rows, w0 : w0 + 256], put_first)
            kv_part = dot(kv_all[rows, w0 : w0 + 256], put_first) + dot(
                kv_all[rows, WIDTH + w0 : WIDTH + w0 + 256], put_second
            )
            kv_part = jnp.where(lane128 >= 96, 1.0, kv_part)
            msg[h, :, 0:128] = kv_part.astype(BF16)
            msg[h, :, 128:256] = q_part.astype(BF16)

    @pl.when(core == 1)
    def _():
        pl.semaphore_wait(barrier, 36)

    def a_copy(k):
        h = seat(k)
        return remote(msg.at[h], recv_a.at[s], a_send.at[k], a_recv, g, 2 * h + 1)

    a_local = pltpu.make_async_copy(msg.at[chip], recv_a.at[s], a_recv)

    def a_all(act):
        each(0, 8, lambda k: act(a_copy(k)))
        each(9, 16, lambda k: act(a_copy(k)))

        @pl.when(core == 0)
        def _():
            act(a_copy(8))

    a_all(lambda c: c.start())

    @pl.when(core == 1)
    def _():
        a_local.start()

    send_across = remote(emb.at[0], emb.at[2], emb_send.at[0], emb_recv.at[0], g, across)
    send_sibling = remote(emb.at[0], emb.at[1], emb_send.at[1], emb_recv.at[1], g, sibling)
    send_on = remote(emb.at[2], emb.at[3], emb_send.at[2], emb_recv.at[2], g, sibling)

    def tell(sem, grp):
        pl.semaphore_signal(sem, inc=1, device_id=(grp, s), device_id_type=MESH)

    @pl.when(core == 1)
    def _():
        tell(past, (g + 12) % 16)

    send_across.start()
    send_sibling.start()

    def other_rows(slot):
        for j in range(6):
            cols = slice(256 * j, 256 * j + 256)
            kv_all[ROWS * slot : ROWS * slot + ROWS, cols] = dot(
                emb[slot], wq[:, WIDTH + 256 * j : WIDTH + 256 * j + 256]
            ).astype(BF16)

    send_sibling.wait_recv()
    other_rows(1)

    @pl.when(core == 1)
    def _():
        pl.semaphore_wait(past, 1)

    def pass_on():
        w1_wait(1)
        w1_copy(3, 1).start()

    @pl.when(core == 0)
    def _():
        wy_start(0)

    bringing(1, pass_on)
    wx_start(1)
    bringing(3, lambda: w1_wait(3))
    wx_start(3)

    e_own = chip // 8

    def kv3_copy(k):
        block = kv3.at[y]
        return remote(block, block, kv3_send.at[k], kv3_recv.at[y], zh * 4 + (y + k) % 4, s)

    def far_copy(k):
        return remote(
            kv3.at[y, pl.ds(0, 32)], far.at[4 * y + zh], far_send.at[k], far_recv.at[zh],
            ((zh + k) % 4) * 4 + y, s,
        )

    def spread_copy(k):
        slots = far.at[pl.ds(4 * y, 4)]
        return remote(slots, slots, far_send.at[k + 4], far_recv.at[4 + y], zh * 4 + (y + k) % 4, s)

    @pl.when(core == 1)
    def _():
        pltpu.make_async_copy(recv_a, recv_a, a_recv).wait()
        spot = iota((128, 512), 0)
        col = iota((128, 512), 1)
        pick = ((spot % 32) * 16 + 4 * e_own + spot // 32 == col).astype(F32).astype(BF16)
        chosen = dot(pick, recv_a[...].reshape(512, 256)).astype(BF16)
        kv3[y] = chosen[:, 0:128]
        q3[...] = chosen[:, 128:256]
        far_copy(2).start()
        far_copy(1).start()
        far_copy(3).start()
        each(1, 4, lambda k: kv3_copy(k).start())

    @pl.when(core == 0)
    def _():
        wf_start(0)
        wy_start(1)
        wy_start(3)

    send_across.wait_recv()
    send_on.start()

    @pl.when(core == 1)
    def _():
        def block(i, carry):
            rows = pl.ds(pl.multiple_of(128 * i, 128), 128)
            flat = recv_a[...].reshape(512, 256)
            queries = recv_a[pl.ds(8 * i, 8)][:, :, 128:256].reshape(128, 128)
            mixed, level = attend(queries, flat[:, 0:128])
            out2[rows, :] = jnp.where(lane128 < 48, level, mixed)
            return carry

        lax.fori_loop(0, 4, block, 0)

    bringing(2, lambda: w1_wait(2))
    wx_start(2)

    @pl.when(core == 0)
    def _():
        wf_start(1)
        wf_start(3)

    other_rows(2)
    send_on.wait_recv()
    other_rows(3)

    @pl.when(core == 0)
    def _():
        wy_start(2)
        w3_start(0)

    def first_branch(pair, carry):
        heads_of(2 * pair)
        heads_of(2 * pair + 1)
        return carry

    def heads_of(rho):
        b = (rho + 5) // 8
        off = 48 * rho - 128 * b
        lane = iota((1, 256), 1)
        mine = (lane >= off) & (lane < off + 48)
        keep = mine.astype(F32).astype(BF16)
        for e in range(2):
            w0 = 384 * e + 128 * b
            win = pl.ds(pl.multiple_of(w0, 128), 256)
            win_v = pl.ds(pl.multiple_of(WIDTH + w0, 128), 256)
            top, weights = soft(dot_nt(q_own[:, win] * keep, kv_all[:, win]))
            total = jnp.sum(weights, axis=1, keepdims=True)
            mixed = dot(weights.astype(BF16), kv_all[:, win_v]) * (1.0 / total)
            att[:, win] = jnp.where(mine, mixed, att[:, win])
            lse[rho + 8 * e] = jnp.broadcast_to(top * SCALE + jnp.log2(total), (ROWS, 128))

    @pl.when(core == 0)
    def _():
        wf_start(2)
        w3_start(1)
        w3_start(3)
        lax.fori_loop(0, 1, first_branch, 0)
        w3_start(2)
        lax.fori_loop(1, 2, first_branch, 0)

    def c_copy(k):
        there = 2 * seat(k // 2) + 1 - k % 2
        return remote(msg_c.at[there], recv_c.at[chip], c_send.at[k], c_recv, g, there)

    def c_all(act):
        each(0, 16, lambda k: act(c_copy(k)))
        each(17, 32, lambda k: act(c_copy(k)))

    @pl.when(core == 1)
    def _():
        each(1, 4, lambda k: pltpu.make_async_copy(kv3.at[0], kv3.at[0], kv3_recv.at[(y + k) % 4]).wait())
        mixed3, level3 = attend(q3[...], kv3[...].reshape(512, 128))

        def fold(m, a, l):
            rows = pl.ds(4 * e_own + m, 32, stride=16)
            held = out2[rows, :]
            a, l = merge(held, held[:, 0:1], a, l)
            out2[rows, :] = jnp.where(lane128 < 48, l, a)

        for m in range(4):
            fold(m, mixed3[32 * m : 32 * m + 32], level3[32 * m : 32 * m + 32])
        far[4 * y + zh] = kv3[y, 0:32, :]
        lax.fori_loop(0, 1, first_branch, 0)
        each(1, 4, lambda k: pltpu.make_async_copy(far.at[0], far.at[0], far_recv.at[(zh + k) % 4]).wait())
        each(1, 4, lambda k: spread_copy(k).start())
        lax.fori_loop(1, 2, first_branch, 0)
        each(1, 4, lambda k: pltpu.make_async_copy(
            far.at[pl.ds(0, 4)], far.at[pl.ds(0, 4)], far_recv.at[4 + (y + k) % 4]).wait())
        mixed4, level4 = attend(q3[0:32, :], far[...].reshape(512, 128))
        fold(0, mixed4, level4)
        done = out2[...]
        level = done[:, 0:1]
        high = level.astype(BF16).astype(F32)
        mid = (level - high).astype(BF16).astype(F32)
        low = level - high - mid
        coded = jnp.where(lane128 == 0, high, jnp.where(lane128 == 1, mid, jnp.where(lane128 == 2, low, done)))
        msg_c[...] = coded.astype(BF16).reshape(32, 16, 128)
        c_all(lambda c: c.start())
        pltpu.make_async_copy(msg_c.at[s], recv_c.at[chip], c_recv).start()

    lax.fori_loop(2, 4, first_branch, 0)

    pltpu.make_async_copy(recv_c, recv_c, c_recv).wait()
    for rho in range(8):
        base = 128 * (rho >= 3)
        off = 48 * rho - base
        src_row = iota((128, 256), 0)
        dst_lane = iota((128, 256), 1)
        put_back = ((src_row - 48 + off == dst_lane) & (src_row >= 48) & (src_row < 96)).astype(F32).astype(BF16)
        add_up = (src_row < 3).astype(F32).astype(BF16)
        lane = iota((1, 256), 1)
        mine = (lane >= off) & (lane < off + 48)
        rows = slice(16 * rho, 16 * rho + 16)
        for e in range(2):
            h = rho + 8 * e
            w0 = 384 * e + base
            other = dot(recv_c[h], put_back)
            level = dot(recv_c[h], add_up)
            own_level = lse[h, rows, 0:1]
            held = att[rows, w0 : w0 + 256]
            share = 1.0 / (1.0 + jnp.exp2(own_level - level))
            att[rows, w0 : w0 + 256] = jnp.where(mine, held + (other - held) * share, held)

    back = (row_order(iota((ROWS, ROWS), 1)) == iota((ROWS, ROWS), 0)).astype(F32).astype(BF16)
    attended = dot(back, att[...].astype(BF16)).astype(BF16)

    @pl.when(core == 1)
    def _():
        each(0, 4, lambda i: w3_copy(i).wait_recv())

    for j in range(3):
        cols = slice(256 * j, 256 * j + 256)
        out_ref[:, cols] = dot(attended, wall[:, :, cols].reshape(WIDTH, 256)).astype(BF16)

    send_across.wait_send()
    send_sibling.wait_send()
    send_on.wait_send()
    a_all(lambda c: c.wait_send())

    @pl.when(core == 1)
    def _():
        each(1, 4, lambda k: kv3_copy(k).wait_send())
        each(1, 4, lambda k: far_copy(k).wait_send())
        each(1, 4, lambda k: spread_copy(k).wait_send())
        c_all(lambda c: c.wait_send())

    @pl.when(core == 0)
    def _():
        each(0, 4, lambda i: w3_copy(i).wait_send())

        for step in range(4):
            for way in range(2):
                wy_copy(step, way).wait_send()
                wf_copy(step, way).wait_send()

    def w1_left():
        w1_copy(1, 0).wait_send()
        w1_copy(3, 0).wait_send()

    bringing(0, w1_left)
    bringing(1, lambda: w1_copy(3, 1).wait_send())
    for step in range(4):
        bringing(step, lambda step=step: each(1, 4, lambda k: wx_copy(step, k).wait_send()))


def shards(tokens, tile_pos, w_qkv, w_out):
    dma = pltpu.SemaphoreType.DMA
    in_hbm = pl.BlockSpec(memory_space=pltpu.HBM)
    return pl.pallas_call(
        kernel,
        out_shape=jax.ShapeDtypeStruct((ROWS, WIDTH), BF16),
        in_specs=[in_hbm] * 4,
        out_specs=pl.BlockSpec(memory_space=pltpu.VMEM),
        scratch_shapes=[
            pltpu.VMEM((ROWS, WIDTH), BF16),
            pltpu.VMEM((2, ROWS), jnp.int32),
            pltpu.VMEM((WIDTH, 3 * WIDTH), BF16),
            pltpu.VMEM((4, ROWS, WIDTH), BF16),
            pltpu.VMEM((ROWS, WIDTH), BF16),
            pltpu.VMEM((4 * ROWS, 2 * WIDTH), BF16),
            pltpu.VMEM((HEADS, 16, 256), BF16),
            pltpu.VMEM((32, 16, 256), BF16),
            pltpu.VMEM((4, 128, 128), BF16),
            pltpu.VMEM((16, 32, 128), BF16),
            pltpu.VMEM((128, 128), BF16),
            pltpu.VMEM((512, 128), F32),
            pltpu.VMEM((32, 16, 128), BF16),
            pltpu.VMEM((HEADS, 16, 128), BF16),
            pltpu.VMEM((ROWS, WIDTH), F32),
            pltpu.VMEM((HEADS, ROWS, 128), F32),
            pltpu.VMEM((48, 16, WIDTH), BF16),
            dma((6,)), dma((3,)), dma((3,)), dma((16,)), dma,
            dma((4,)), dma((4,)), dma((8,)), dma((8,)), dma((32,)), dma,
            dma((5,)), dma((4,)), dma((4, 4)), dma((4,)), dma((4, 2)), dma((4, 2)), dma((4, 2)), dma((4, 2)), dma((4,)), dma((4,)),
            pltpu.SemaphoreType.REGULAR,
        ],
        compiler_params=pltpu.CompilerParams(
            collective_id=0, has_side_effects=True, vmem_limit_bytes=60 * 1024 * 1024
        ),
        name="dilated_attention",
    )(tokens, tile_pos, w_qkv, w_out)


def solution(mesh):
    placed = (P(("grp", "seq"), None), P(None, ("grp", "seq")), P(), P("grp", None))
    return jax.shard_map(
        shards, mesh=mesh, in_specs=placed, out_specs=P(("grp", "seq"), None), check_vma=False
    )
```
